768 devices in a mesh: band: 8 (over y), lon: 96 (over x, z, core).
Axes of the slice: x: 4, y: 8, z: 12, core: 2. Of those that a mesh axis runs over, the one named last changes fastest.
Arguments:
- grid_latent: bfloat16 [786432, 512], P(('band', 'lon')), may hold values from -6 to 6
- mesh_latent: bfloat16 [98304, 512], P(('band', 'lon')), may hold values from -6 to 6
- mesh_cotangent: bfloat16 [98304, 512], P(('band', 'lon')), may hold values from -6 to 6
- w_grid: bfloat16 [512, 512], replicated, may hold values from -0.25 to 0.25
- w_mesh: bfloat16 [512, 512], replicated, may hold values from -0.25 to 0.25
- w_out: bfloat16 [512, 512], replicated, may hold values from -0.25 to 0.25
- edge_source: int32 [1572864], P(('band', 'lon')), may hold values from 0 to 1023
- edge_target: int32 [1572864], P(('band', 'lon')), may hold values from 0 to 98303, as said below
- edge_count: int32 [768], P(('band', 'lon')), may hold values from 256 to 2048, as said below
Outputs:
- grid_grad: bfloat16 [786432, 512], P(('band', 'lon'))
- mesh_grad: bfloat16 [98304, 512], P(('band', 'lon'))
- weight_grads: float32 [1536, 512], P('lon')
The draws below stay inside these ranges and needn't reach their ends.
Inputs may be any that keep to these rules, and one draw needn't show every extreme that they name: `edge_target`: the mesh node of a slot of device block d lies in mesh block d or in the next lon block of the same band, with wrap: rows ((band index) * 96 + (lon index + 0 or 1) % 96) * 128 to that plus 128 - 1. `edge_count`: some device has exactly 2048 live slots.
All inputs are finite; a program needn't handle non-finite values.
Results may differ from the reference program's by a relative error of at most 0.015.
Values may be sent and summed in bfloat16 or wider, within the bound.
A program may use at most 32 MiB of HBM per device.

```python
import jax
import jax.numpy as jnp
from jax import lax

D = 512
G_DEV = 1024
MB = 128
EDGE_DEV = 2048
GRID = 786432
MESH = 98304
EDGES = 1572864
N_BAND = 8
N_LON = 96


def draw_edge_target(key, part):
    key = jax.random.fold_in(key, 11)
    first_key, second_key = jax.random.split(key)
    position = jnp.arange(EDGES, dtype=jnp.int32)
    device = position // EDGE_DEV
    band_index = device // N_LON
    lon_index = device % N_LON
    step_east = jax.random.randint(first_key, (EDGES,), 0, 2, dtype=jnp.int32)
    row_index = jax.random.randint(second_key, (EDGES,), 0, MB, dtype=jnp.int32)
    block = band_index * N_LON + (lon_index + step_east) % N_LON
    return (block * MB + row_index).astype(jnp.int32)


def draw_edge_count(key, part):
    key = jax.random.fold_in(key, 23)
    light_key, heavy_key, pick_key = jax.random.split(key, 3)
    devices = N_BAND * N_LON
    device = jnp.arange(devices, dtype=jnp.int32)
    band_index = device // N_LON
    polar = (band_index == 0) | (band_index == N_BAND - 1)
    light = jax.random.randint(light_key, (devices,), EDGE_DEV // 8, EDGE_DEV // 2 + 1, dtype=jnp.int32)
    heavy = jax.random.randint(heavy_key, (devices,), EDGE_DEV // 2, EDGE_DEV + 1, dtype=jnp.int32)
    counts = jnp.where(polar, heavy, light)
    chosen = jax.random.randint(pick_key, (), 0, devices, dtype=jnp.int32)
    return counts.at[chosen].set(EDGE_DEV).astype(jnp.int32)


def touch_ends(array, own_key, low, largest):
    longest = array.shape.index(max(array.shape))
    spots = []
    for shift in (0, 1):
        where = [jax.random.randint(jax.random.fold_in(own_key, axis), (), 0, length) for axis, length in enumerate(array.shape)]
        where[longest] = (where[longest] + shift) % array.shape[longest]
        spots.append(tuple(where))
    return array.at[spots[0]].set(low).at[spots[1]].set(largest)


def levels(stream_key, dims, cuts, least, top_value):
    gain = 1.0
    for dim, parts in cuts:
        steps = jax.random.uniform(jax.random.fold_in(jax.random.fold_in(stream_key, 6), dim), (parts,), jnp.float32, least / len(cuts), top_value / len(cuts))
        gain = gain * jnp.repeat(jnp.exp(steps), dims[dim] // parts).reshape((-1,) + (1,) * (len(dims) - 1 - dim))
    return gain


def scatter_about(key, shape, scale, bound, cuts=(), held_as=jnp.bfloat16):
    values = jax.random.normal(key, shape, jnp.float32) * scale
    if len(cuts) > 0:
        values = levels(key, shape, cuts, -0.22, 0.18) * values
    return jnp.clip(values, min=-bound, max=bound).astype(held_as)


def setup_inputs(seed: int = 0) -> dict:
    arg_keys = jax.random.split(jax.random.key(seed), 10)
    return {
        "grid_latent": scatter_about(arg_keys[0], (GRID, D), 1.0, 6.0, ((0, 768),)),
        "mesh_latent": scatter_about(arg_keys[1], (MESH, D), 1.0, 6.0, ((0, 768),)),
        "mesh_cotangent": scatter_about(arg_keys[2], (MESH, D), 1.0, 6.0, ((0, 768),)),
        "w_grid": scatter_about(arg_keys[3], (D, D), D ** -0.5, 0.25),
        "w_mesh": scatter_about(arg_keys[4], (D, D), D ** -0.5, 0.25),
        "w_out": scatter_about(arg_keys[5], (D, D), D ** -0.5, 0.25),
        "edge_source": touch_ends(jax.random.randint(arg_keys[6], (EDGES,), 0, G_DEV), jax.random.fold_in(arg_keys[6], 1), 0, G_DEV - 1).astype(jnp.int32),
        "edge_target": draw_edge_target(jax.random.fold_in(arg_keys[9], 71), 0),
        "edge_count": draw_edge_count(jax.random.fold_in(arg_keys[9], 71), 0),
    }


def silu_slope(values):
    sig = jax.nn.sigmoid(values)
    return sig * (1.0 + values * (1.0 - sig))


def reference(grid_latent, mesh_latent, mesh_cotangent, w_grid, w_mesh, w_out, edge_source, edge_target, edge_count):
    devices = N_BAND * N_LON
    proj_grid = jnp.dot(grid_latent, w_grid, preferred_element_type=jnp.float32).astype(jnp.bfloat16)
    proj_mesh = jnp.dot(mesh_latent, w_mesh, preferred_element_type=jnp.float32).astype(jnp.bfloat16)
    slot_ids = jnp.arange(EDGE_DEV, dtype=jnp.int32)

    def step(carry, inputs):
        mesh_acc, out_acc = carry
        grid_rows, sources, targets, count = inputs
        alive = slot_ids < count
        preact = grid_rows[sources].astype(jnp.float32) + proj_mesh[targets].astype(jnp.float32)
        activation = jax.nn.silu(preact).astype(jnp.bfloat16)
        edge_cot = jnp.where(alive[:, None], mesh_cotangent[targets], jnp.zeros((), jnp.bfloat16))
        out_acc = out_acc + lax.dot_general(activation, edge_cot, (((0,), (0,)), ((), ())), preferred_element_type=jnp.float32)
        grad_act = lax.dot_general(edge_cot, w_out, (((1,), (1,)), ((), ())), preferred_element_type=jnp.float32)
        grad_pre = (grad_act * silu_slope(preact)).astype(jnp.bfloat16).astype(jnp.float32)
        grid_part = jax.ops.segment_sum(grad_pre, sources, num_segments=G_DEV)
        mesh_acc = mesh_acc.at[targets].add(grad_pre)
        return (mesh_acc, out_acc), grid_part

    initial = (jnp.zeros((MESH, D), jnp.float32), jnp.zeros((D, D), jnp.float32))
    inputs = (proj_grid.reshape(devices, G_DEV, D), edge_source.reshape(devices, EDGE_DEV),
              edge_target.reshape(devices, EDGE_DEV), edge_count)
    (mesh_acc, grad_w_out), grid_parts = lax.scan(step, initial, inputs)
    grad_proj_grid = grid_parts.reshape(GRID, D).astype(jnp.bfloat16)
    grad_proj_mesh = mesh_acc.astype(jnp.bfloat16)
    grid_grad = lax.dot_general(grad_proj_grid, w_grid, (((1,), (1,)), ((), ())), preferred_element_type=jnp.float32).astype(jnp.bfloat16)
    mesh_grad = lax.dot_general(grad_proj_mesh, w_mesh, (((1,), (1,)), ((), ())), preferred_element_type=jnp.float32).astype(jnp.bfloat16)
    grad_w_grid = lax.dot_general(grid_latent, grad_proj_grid, (((0,), (0,)), ((), ())), preferred_element_type=jnp.float32)
    grad_w_mesh = lax.dot_general(mesh_latent, grad_proj_mesh, (((0,), (0,)), ((), ())), preferred_element_type=jnp.float32)
    weight_grads = jnp.concatenate([grad_w_grid, grad_w_mesh, grad_w_out], axis=0)
    return (grid_grad, mesh_grad, weight_grads)
```

```python
import jax
import jax.numpy as jnp
from jax import lax
from jax.experimental import pallas as pl
from jax.experimental.pallas import tpu as pltpu
from jax.sharding import PartitionSpec as P

MESH = pl.DeviceIdType.MESH
BF16 = jnp.bfloat16
F32 = jnp.float32

D = 512
HALF = 256
GRID_ROWS = 1024
MESH_ROWS = 128
TABLE = 2 * MESH_ROWS
SLOTS = 2048
LANES = 128
NX, NY, NZ, NC = 4, 8, 12, 2
N_LON = NX * NZ * NC
GRID_TYPE, MESH_TYPE, OUT_TYPE = 0, 1, 2


def dot(a, b):
    return lax.dot_general(a, b, (((1,), (0,)), ((), ())), preferred_element_type=F32)


def dot_bt(a, b):
    return lax.dot_general(a, b, (((1,), (1,)), ((), ())), preferred_element_type=F32)


def lon_of(x, z, c):
    return (x * NZ + z) * NC + c


def piece_rows(kind, c, x):
    if kind == GRID_TYPE:
        return ((1 - c) * NX + x) * 64
    if kind == MESH_TYPE:
        return (c * NX + x) * 64
    return c * HALF + ((x + 1) % NX) * 64


def owner_of(x, z, c, half):
    kind, j = z // 4, z % 4
    grid = (1 - c) * 16 + x * 4 + j
    mesh = 32 + c * 16 + x * 4 + j
    out = 64 + 16 * half + 4 * ((x + 1) % NX) + j
    return jnp.where(kind == 0, grid, jnp.where(kind == 1, mesh, out))


def summer_of(lon, which):
    kind = lon // 32
    k = lon % 32
    grid = lon_of((k // 4) % NX, k % 4, 1 - k // 16)
    mesh = lon_of((k // 4) % NX, 4 + k % 4, k // 16)
    b = lon % 16
    out = lon_of((b // 4 + 3) % NX, 8 + b % 4, which)
    return jnp.where(kind == 0, grid, jnp.where(kind == 1, mesh, out))


def kernel(
    gl_hbm, ml_hbm, ct_hbm, wg_hbm, wm_hbm, wo_hbm, src_hbm, tgt_hbm, cnt_hbm,
    gg_hbm, mg_hbm, wgrad_hbm,
    gl, glt, wg, wm, wo, ml, mlt, ct, src, tgt, cnt,
    pick, pickt, table, gtable, actgp, gpg, gg, mg,
    mine, tosend, west,
    piece, core_in, mid, x_in, low, z_in, last, y_in, wout,
    load_sem, store_sem,
    east_send, east_recv, west_send, west_recv,
    core_send, core_recv, x_send, x_recv, z_send, z_recv, y_send, y_recv,
):
    band = lax.axis_index("band")
    lon = lax.axis_index("lon")
    x = lon // (NZ * NC)
    z = (lon // NC) % NZ
    c = lon % NC
    kind = z // 4
    own_kind = lon // 32
    to_west = (band, (lon + N_LON - 1) % N_LON)
    to_east = (band, (lon + 1) % N_LON)
    mate = (band, lon_of(x, z, 1 - c))

    def load(i, source, target):
        return pltpu.make_async_copy(source, target, load_sem.at[i])

    loads = [
        load(0, ml_hbm, ml.at[pl.ds(0, MESH_ROWS)]),
        load(1, ct_hbm, ct.at[pl.ds(0, MESH_ROWS)]),
        load(2, src_hbm, src),
        load(3, tgt_hbm, tgt),
        load(4, cnt_hbm, cnt),
        load(5, gl_hbm, gl),
        load(6, wg_hbm, wg),
        load(7, wm_hbm, wm),
        load(8, wo_hbm, wo),
    ]
    for copy in loads:
        copy.start()

    barrier = pltpu.get_barrier_semaphore()

    def greet(device):
        pl.semaphore_signal(barrier, inc=1, device_id=device, device_id_type=MESH)

    greet(to_west)
    greet(to_east)
    greet(mate)
    for d in range(1, NX):
        greet((band, lon_of((x + d) % NX, z, c)))

    def greet_z(d, carry):
        greet((band, lon_of(x, (z + d) % NZ, c)))
        return carry

    lax.fori_loop(1, NZ, greet_z, 0)

    def greet_y(y, carry):
        greet((y, owner_of(x, z, c, 0)))
        greet((y, summer_of(lon, 0)))

        @pl.when(kind == OUT_TYPE)
        def _():
            greet((y, owner_of(x, z, c, 1)))

        @pl.when(own_kind == OUT_TYPE)
        def _():
            greet((y, summer_of(lon, 1)))

        return carry

    lax.fori_loop(0, NY, greet_y, 0)
    loads[0].wait()
    loads[1].wait()
    pl.semaphore_wait(
        barrier,
        3 + (NX - 1) + (NZ - 1) + 2 * NY
        + jnp.where(kind == OUT_TYPE, NY, 0) + jnp.where(own_kind == OUT_TYPE, NY, 0),
    )

    def east_copy(i, ref):
        return pltpu.make_async_remote_copy(
            src_ref=ref.at[pl.ds(0, MESH_ROWS)],
            dst_ref=ref.at[pl.ds(MESH_ROWS, MESH_ROWS)],
            send_sem=east_send.at[i],
            recv_sem=east_recv.at[i],
            device_id=to_west,
            device_id_type=MESH,
        )

    def west_copy(half):
        return pltpu.make_async_remote_copy(
            src_ref=tosend.at[half],
            dst_ref=west.at[half],
            send_sem=west_send.at[half],
            recv_sem=west_recv.at[half],
            device_id=to_east,
            device_id_type=MESH,
        )

    def core_copy(half, t):
        return pltpu.make_async_remote_copy(
            src_ref=piece.at[half, t, 1 - c],
            dst_ref=core_in.at[half, t],
            send_sem=core_send.at[half, t],
            recv_sem=core_recv.at[half, t],
            device_id=mate,
            device_id_type=MESH,
        )

    def x_copy(half, t, d):
        there = (x + d) % NX
        return pltpu.make_async_remote_copy(
            src_ref=mid.at[half, t, there],
            dst_ref=x_in.at[half, t, d - 1],
            send_sem=x_send.at[half, t, d - 1],
            recv_sem=x_recv.at[half, t, d - 1],
            device_id=(band, lon_of(there, z, c)),
            device_id_type=MESH,
        )

    def z_copy(half, there):
        slot = (there + NZ - z + NZ - 1) % NZ
        return pltpu.make_async_remote_copy(
            src_ref=low.at[half, there],
            dst_ref=z_in.at[half, slot],
            send_sem=z_send.at[half],
            recv_sem=z_recv.at[half],
            device_id=(band, lon_of(x, there, c)),
            device_id_type=MESH,
        )

    def y_copy(half, y):
        side = jnp.where(kind == OUT_TYPE, c, half)
        return pltpu.make_async_remote_copy(
            src_ref=last.at[half],
            dst_ref=y_in.at[side, band],
            send_sem=y_send.at[half],
            recv_sem=y_recv.at[side],
            device_id=(y, owner_of(x, z, c, half)),
            device_id_type=MESH,
        )

    def whole(ref, send, recv):
        return pltpu.make_async_remote_copy(
            src_ref=ref, dst_ref=ref, send_sem=send, recv_sem=recv,
            device_id=mate, device_id_type=MESH,
        )

    east_copy(0, ml).start()
    east_copy(1, ct).start()

    for i in (2, 3, 4):
        loads[i].wait()

    slot = lax.broadcasted_iota(jnp.int32, (SLOTS // LANES, LANES), 0) * LANES
    slot = slot + lax.broadcasted_iota(jnp.int32, (SLOTS // LANES, LANES), 1)
    target = tgt[...]
    start = (band * N_LON + lon) * MESH_ROWS
    here = (target >= start) & (target < start + MESH_ROWS)
    row = jnp.where(here, target - start, MESH_ROWS + (target & (MESH_ROWS - 1)))
    alive = slot < cnt[...]
    tgt[...] = jnp.where(alive, row, -1) + GRID_ROWS

    def build(r, carry):
        s = src[pl.ds(r, 1), :]
        t = tgt[pl.ds(r, 1), :]
        columns = pl.ds(pl.multiple_of(r * LANES, LANES), LANES)
        down = lax.broadcasted_iota(jnp.int32, (LANES, LANES), 0)
        across = lax.broadcasted_iota(jnp.int32, (LANES, LANES), 1)
        sb = jnp.broadcast_to(s, (LANES, LANES))
        tb = jnp.broadcast_to(jnp.where(t < GRID_ROWS, -1, t), (LANES, LANES))
        st = sb.T
        tt = tb.T
        for k in range((GRID_ROWS + TABLE) // LANES):
            one = (sb if k < GRID_ROWS // LANES else tb) == down + k * LANES
            pickt[k * LANES:(k + 1) * LANES, columns] = jnp.where(one, 1.0, 0.0).astype(BF16)
            one = (st if k < GRID_ROWS // LANES else tt) == across + k * LANES
            pick[columns, k * LANES:(k + 1) * LANES] = jnp.where(one, 1.0, 0.0).astype(BF16)
        return carry

    lax.fori_loop(0, SLOTS // LANES, build, 0)

    loads[5].wait()
    loads[6].wait()

    def turn(i, carry):
        rows = pl.ds(pl.multiple_of(i * 256, 256), 256)
        glt[:, rows] = gl[rows, :].T
        return carry

    lax.fori_loop(0, GRID_ROWS // 256, turn, 0)

    def put(half, t, values):
        values = values.astype(BF16)
        for cc in range(NC):
            for xx in range(NX):
                first = piece_rows(t, cc, xx)
                piece[half, t, cc, xx] = values[first:first + 64]
        core_copy(half, t).start()

    def after_core(half, t):
        core_copy(half, t).wait_recv()
        for xx in range(NX):
            total = piece[half, t, c, xx].astype(F32) + core_in[half, t, xx].astype(F32)
            mid[half, t, xx] = total.astype(BF16)
        for d in range(1, NX):
            x_copy(half, t, d).start()

    def after_x(half, t):
        for d in range(1, NX):
            x_copy(half, t, d).wait_recv()
        total = mid[half, t, x].astype(F32)
        for d in range(1, NX):
            total = total + x_in[half, t, d - 1].astype(F32)
        total = total.astype(BF16)
        for j in range(4):
            low[half, t * 4 + j] = total[j * 16:(j + 1) * 16]
        for j in range(4):
            @pl.when(z != t * 4 + j)
            def _():
                z_copy(half, t * 4 + j).start()

    def after_z(half):
        whole(z_in.at[half], z_send.at[half], z_recv.at[half]).wait_recv()
        total = low[half, z].astype(F32)
        for s in range(NZ - 1):
            total = total + z_in[half, s].astype(F32)
        last[half] = total.astype(BF16)

        def send(y, carry):
            y_copy(half, y).start()
            return carry

        lax.fori_loop(0, NY, send, 0)

    def tables(half):
        columns = slice(half * HALF, (half + 1) * HALF)

        def project(i, carry):
            rows = pl.ds(pl.multiple_of(i * 256, 256), 256)
            table[rows, :] = dot(gl[rows, :], wg[:, columns]).astype(BF16)
            return carry

        lax.fori_loop(0, GRID_ROWS // 256, project, 0)
        if half == 0:
            loads[7].wait()
            loads[8].wait()
            east_copy(0, ml).wait_recv()
            east_copy(1, ct).wait_recv()
            mlt[...] = ml[...].T
        table[GRID_ROWS:, :] = dot(ml[...], wm[:, columns]).astype(BF16)
        gtable[...] = dot_bt(ct[...], wo[columns, :]).astype(BF16)

    def edges(half):
        def step(i, carry):
            rows = pl.ds(pl.multiple_of(i * 256, 256), 256)
            pre = dot(pick[rows, :], table[...])
            grad = dot(pick[rows, GRID_ROWS:], gtable[...])
            sig = 0.5 * jnp.tanh(0.5 * pre) + 0.5
            act = pre * sig
            actgp[rows, :HALF] = act.astype(BF16)
            actgp[rows, HALF:] = (grad * (sig + act * (1.0 - sig))).astype(BF16)
            return carry

        lax.fori_loop(0, SLOTS // 256, step, 0)

    def mesh_side(half):
        sums = dot(pickt[GRID_ROWS:, :], actgp[...])
        terms = sums[:, HALF:]
        mine[half] = terms[:MESH_ROWS]
        termsb = terms.astype(BF16)
        tosend[half] = termsb[MESH_ROWS:]
        west_copy(half).start()
        acts = sums[:, :HALF].T.astype(BF16)
        out = dot(acts, ct[...])
        put(half, OUT_TYPE, jnp.concatenate([out[:, :HALF], out[:, HALF:]], axis=0))
        put(half, MESH_TYPE, dot(mlt[...], termsb))

    def grid_side(half):
        columns = slice(half * HALF, (half + 1) * HALF)

        def step(i, carry):
            rows = pl.ds(pl.multiple_of(i * 256, 256), 256)
            gpg[rows, columns] = dot(pickt[rows, :], actgp[:, HALF:]).astype(BF16)
            return carry

        lax.fori_loop(0, GRID_ROWS // 256, step, 0)

    def grid_weights(half):
        columns = slice(half * HALF, (half + 1) * HALF)
        put(half, GRID_TYPE, dot(glt[...], gpg[:, columns]))

    def grid_grads(first):
        def step(i, carry):
            rows = pl.ds(pl.multiple_of(i * 256, 256), 256)
            gg[rows, :] = dot_bt(gpg[rows, :], wg[...]).astype(BF16)
            return carry

        lax.fori_loop(first, first + 2, step, 0)

    def store(i, source, goal):
        return pltpu.make_async_copy(source, goal, store_sem.at[i])

    tables(0)
    edges(0)
    mesh_side(0)
    grid_side(0)
    grid_weights(0)
    tables(1)
    for t in (OUT_TYPE, MESH_TYPE, GRID_TYPE):
        after_core(0, t)
    edges(1)
    for t in (OUT_TYPE, MESH_TYPE, GRID_TYPE):
        after_x(0, t)
    mesh_side(1)
    grid_side(1)
    after_core(1, OUT_TYPE)
    after_core(1, MESH_TYPE)
    grid_weights(1)
    after_z(0)
    after_x(1, OUT_TYPE)
    after_x(1, MESH_TYPE)
    after_core(1, GRID_TYPE)
    grid_grads(0)
    after_x(1, GRID_TYPE)
    grid_grads(2)
    store(0, gg, gg_hbm).start()
    for half in range(2):
        west_copy(half).wait_recv()
    total = jnp.zeros((MESH_ROWS, D), F32)
    for half in range(2):
        columns = slice(half * HALF, (half + 1) * HALF)
        sums = (mine[half] + west[half].astype(F32)).astype(BF16)
        total = total + dot_bt(sums, wm[:, columns])
    mg[...] = total.astype(BF16)
    store(1, mg, mg_hbm).start()
    after_z(1)
    for side in range(2):
        whole(y_in.at[side], y_send.at[side], y_recv.at[side]).wait_recv()
        total = y_in[side, 0].astype(F32)
        for s in range(1, NY):
            total = total + y_in[side, s].astype(F32)
        wout[:, side * HALF:(side + 1) * HALF] = total
    store(2, wout, wgrad_hbm).start()

    east_copy(0, ml).wait_send()
    east_copy(1, ct).wait_send()
    for half in range(2):
        west_copy(half).wait_send()
        for t in range(3):
            core_copy(half, t).wait_send()
            for d in range(1, NX):
                x_copy(half, t, d).wait_send()
        whole(z_in.at[half], z_send.at[half], z_recv.at[half]).wait_send()
        whole(y_in.at[half], y_send.at[half], y_recv.at[half]).wait_send()
    store(0, gg, gg_hbm).wait()
    store(1, mg, mg_hbm).wait()
    store(2, wout, wgrad_hbm).wait()


def on_device(
    grid_latent, mesh_latent, mesh_cotangent, w_grid, w_mesh, w_out, edge_source, edge_target, edge_count
):
    edges = (SLOTS // LANES, LANES)
    count = jnp.broadcast_to(edge_count.reshape(1, 1), edges)
    dma = pltpu.SemaphoreType.DMA
    vmem = pltpu.VMEM
    return pl.pallas_call(
        kernel,
        out_shape=(
            jax.ShapeDtypeStruct((GRID_ROWS, D), BF16),
            jax.ShapeDtypeStruct((MESH_ROWS, D), BF16),
            jax.ShapeDtypeStruct((16, D), F32),
        ),
        in_specs=[pl.BlockSpec(memory_space=pl.ANY)] * 9,
        out_specs=[pl.BlockSpec(memory_space=pl.ANY)] * 3,
        scratch_shapes=[
            vmem((GRID_ROWS, D), BF16),
            vmem((D, GRID_ROWS), BF16),
            vmem((D, D), BF16),
            vmem((D, D), BF16),
            vmem((D, D), BF16),
            vmem((TABLE, D), BF16),
            vmem((D, TABLE), BF16),
            vmem((TABLE, D), BF16),
            vmem(edges, jnp.int32),
            vmem(edges, jnp.int32),
            vmem(edges, jnp.int32),
            vmem((SLOTS, GRID_ROWS + TABLE), BF16),
            vmem((GRID_ROWS + TABLE, SLOTS), BF16),
            vmem((GRID_ROWS + TABLE, HALF), BF16),
            vmem((TABLE, HALF), BF16),
            vmem((SLOTS, D), BF16),
            vmem((GRID_ROWS, D), BF16),
            vmem((GRID_ROWS, D), BF16),
            vmem((MESH_ROWS, D), BF16),
            vmem((2, MESH_ROWS, HALF), F32),
            vmem((2, MESH_ROWS, HALF), BF16),
            vmem((2, MESH_ROWS, HALF), BF16),
            vmem((2, 3, NC, NX, 64, HALF), BF16),
            vmem((2, 3, NX, 64, HALF), BF16),
            vmem((2, 3, NX, 64, HALF), BF16),
            vmem((2, 3, NX - 1, 64, HALF), BF16),
            vmem((2, NZ, 16, HALF), BF16),
            vmem((2, NZ - 1, 16, HALF), BF16),
            vmem((2, 16, HALF), BF16),
            vmem((2, NY, 16, HALF), BF16),
            vmem((16, D), F32),
            dma((9,)),
            dma((3,)),
            dma((2,)),
            dma((2,)),
            dma((2,)),
            dma((2,)),
            dma((2, 3)),
            dma((2, 3)),
            dma((2, 3, NX - 1)),
            dma((2, 3, NX - 1)),
            dma((2,)),
            dma((2,)),
            dma((2,)),
            dma((2,)),
        ],
        compiler_params=pltpu.CompilerParams(
            collective_id=0, has_side_effects=True, vmem_limit_bytes=56 * 1024 * 1024
        ),
        cost_estimate=pl.CostEstimate(flops=17_000_000_000, bytes_accessed=5_000_000, transcendentals=1_000_000),
    )(
        grid_latent, mesh_latent, mesh_cotangent, w_grid, w_mesh, w_out,
        edge_source.reshape(edges), edge_target.reshape(edges), count,
    )


def solution(mesh):
    in_specs = (
        P(("band", "lon"), None),
        P(("band", "lon"), None),
        P(("band", "lon"), None),
        P(),
        P(),
        P(),
        P(("band", "lon")),
        P(("band", "lon")),
        P(("band", "lon")),
    )
    out_specs = (P(("band", "lon"), None), P(("band", "lon"), None), P("lon", None))
    return jax.shard_map(
        on_device, mesh=mesh, in_specs=in_specs, out_specs=out_specs, check_vma=False
    )
```

```python
import jax
import jax.numpy as jnp
from jax import lax
from jax.experimental import pallas as pl
from jax.experimental.pallas import tpu as pltpu
from jax.sharding import PartitionSpec as P

MESH = pl.DeviceIdType.MESH
BF16 = jnp.bfloat16
F32 = jnp.float32

D = 512
GRID_ROWS = 1024
MESH_ROWS = 128
TABLE = 2 * MESH_ROWS
SLOTS = 2048
LANES = 128
NX, NY, NZ, NC = 4, 8, 12, 2
N_LON = NX * NZ * NC
GRID_TYPE, MESH_TYPE, OUT_TYPE = 0, 1, 2
SPOTS = (
    ((0, 0), (0, 1), (0, 2), (1, 0)),
    ((1, 1), (1, 2), (2, 0), (2, 1)),
    ((2, 2), (3, 0), (3, 1), (3, 2)),
)


def dot(a, b):
    return lax.dot_general(a, b, (((1,), (0,)), ((), ())), preferred_element_type=F32)


def dot_bt(a, b):
    return lax.dot_general(a, b, (((1,), (1,)), ((), ())), preferred_element_type=F32)


def lon_of(x, z, c):
    return (x * NZ + z) * NC + c


def spot_z(x, t, j):
    owner_x, group = SPOTS[t][j]
    return 4 * group + (x + NX - owner_x) % NX


def block_row(t, c, x, j):
    return 16 * (lon_of(SPOTS[t][j][0], spot_z(x, t, j), c) - 32 * t)


def kernel(
    gl_hbm, ml_hbm, ct_hbm, wg_hbm, wm_hbm, wo_hbm, src_hbm, tgt_hbm, cnt,
    gg_hbm, mg_hbm, wgrad_hbm,
    gl, glt, wg, wm, wo, ml, mlt, ct, src, tgt,
    pick, pickt, table, mtable, pre, actgp, gpg, gg, mg,
    mine, tosend, west,
    piece, core_in, mid, x_in, low, z_in, last, y_in, wout,
    load_sem, store_sem,
    east_send, east_recv, west_send, west_recv,
    core_send, core_recv, x_send, x_recv, z_send, z_recv, y_send, y_recv,
):
    band = lax.axis_index("band")
    lon = lax.axis_index("lon")
    x = lon // (NZ * NC)
    z = (lon // NC) % NZ
    c = lon % NC
    moved = z % NX != 0
    owner = lon_of((x + NZ - z) % NX, z, c)
    summer = lon_of((x + z) % NX, z, c)
    to_west = (band, (lon + N_LON - 1) % N_LON)
    to_east = (band, (lon + 1) % N_LON)
    mate = (band, lon_of(x, z, 1 - c))

    def load(i, source, target):
        return pltpu.make_async_copy(source, target, load_sem.at[i])

    loads = [
        load(0, src_hbm, src),
        load(1, tgt_hbm, tgt),
        load(2, gl_hbm, gl),
        load(3, wg_hbm, wg),
        load(4, ml_hbm, ml.at[pl.ds(0, MESH_ROWS)]),
        load(5, ct_hbm, ct.at[pl.ds(0, MESH_ROWS)]),
        load(6, wm_hbm, wm),
        load(7, wo_hbm, wo),
    ]
    for copy in loads:
        copy.start()

    barrier = pltpu.get_barrier_semaphore()

    def greet(device):
        pl.semaphore_signal(barrier, inc=1, device_id=device, device_id_type=MESH)

    greet(to_west)
    greet(to_east)
    greet(mate)
    for d in range(1, NX):
        greet((band, lon_of((x + d) % NX, z, c)))

    def greet_z(d, carry):
        greet((band, lon_of(x, (z + d) % NZ, c)))
        return carry

    lax.fori_loop(1, NZ, greet_z, 0)

    def greet_y(d, carry):
        greet(((band + d) % NY, owner))
        greet(((band + d) % NY, summer))
        return carry

    lax.fori_loop(1, NY, greet_y, 0)

    @pl.when(moved)
    def _():
        greet((band, owner))
        greet((band, summer))

    def east_copy(i, ref):
        return pltpu.make_async_remote_copy(
            src_ref=ref.at[pl.ds(0, MESH_ROWS)],
            dst_ref=ref.at[pl.ds(MESH_ROWS, MESH_ROWS)],
            send_sem=east_send.at[i],
            recv_sem=east_recv.at[i],
            device_id=to_west,
            device_id_type=MESH,
        )

    def west_copy():
        return pltpu.make_async_remote_copy(
            src_ref=tosend,
            dst_ref=west,
            send_sem=west_send,
            recv_sem=west_recv,
            device_id=to_east,
            device_id_type=MESH,
        )

    def core_copy(t):
        return pltpu.make_async_remote_copy(
            src_ref=piece.at[t, 1 - c],
            dst_ref=core_in.at[t],
            send_sem=core_send.at[t],
            recv_sem=core_recv.at[t],
            device_id=mate,
            device_id_type=MESH,
        )

    def x_copy(t, d):
        there = (x + d) % NX
        return pltpu.make_async_remote_copy(
            src_ref=mid.at[t, there],
            dst_ref=x_in.at[t, d - 1],
            send_sem=x_send.at[t, d - 1],
            recv_sem=x_recv.at[t, d - 1],
            device_id=(band, lon_of(there, z, c)),
            device_id_type=MESH,
        )

    def z_copy(there):
        slot = (there + NZ - z + NZ - 1) % NZ
        return pltpu.make_async_remote_copy(
            src_ref=low.at[there],
            dst_ref=z_in.at[slot],
            send_sem=z_send,
            recv_sem=z_recv,
            device_id=(band, lon_of(x, there, c)),
            device_id_type=MESH,
        )

    def y_copy(y, i):
        return pltpu.make_async_remote_copy(
            src_ref=last,
            dst_ref=y_in.at[band],
            send_sem=y_send.at[i],
            recv_sem=y_recv.at[i],
            device_id=(y, owner),
            device_id_type=MESH,
        )

    def whole(ref, send, recv):
        return pltpu.make_async_remote_copy(
            src_ref=ref, dst_ref=ref, send_sem=send, recv_sem=recv,
            device_id=mate, device_id_type=MESH,
        )

    loads[0].wait()
    loads[1].wait()
    slot = lax.broadcasted_iota(jnp.int32, (SLOTS // LANES, LANES), 0) * LANES
    slot = slot + lax.broadcasted_iota(jnp.int32, (SLOTS // LANES, LANES), 1)
    target = tgt[...]
    start = (band * N_LON + lon) * MESH_ROWS
    here = (target >= start) & (target < start + MESH_ROWS)
    row = jnp.where(here, target - start, MESH_ROWS + (target & (MESH_ROWS - 1)))
    tgt[...] = jnp.where(slot < cnt[0], row + GRID_ROWS, -1)

    def build(r, carry):
        columns = pl.ds(pl.multiple_of(r * LANES, LANES), LANES)
        down = lax.broadcasted_iota(jnp.int32, (LANES, LANES), 0).astype(jnp.int16)
        across = lax.broadcasted_iota(jnp.int32, (LANES, LANES), 1).astype(jnp.int16)
        sb = jnp.broadcast_to(src[pl.ds(r, 1), :], (LANES, LANES)).astype(jnp.int16)
        tb = jnp.broadcast_to(tgt[pl.ds(r, 1), :], (LANES, LANES)).astype(jnp.int16)
        st = sb.T
        tt = tb.T
        for k in range((GRID_ROWS + TABLE) // LANES):
            one = (sb if k < GRID_ROWS // LANES else tb) == down + jnp.int16(k * LANES)
            pickt[k * LANES:(k + 1) * LANES, columns] = jnp.where(one, jnp.ones((), BF16), jnp.zeros((), BF16))
            one = (st if k < GRID_ROWS // LANES else tt) == across + jnp.int16(k * LANES)
            pick[columns, k * LANES:(k + 1) * LANES] = jnp.where(one, jnp.ones((), BF16), jnp.zeros((), BF16))
        return carry

    lax.fori_loop(0, SLOTS // LANES, build, 0)

    loads[2].wait()
    loads[3].wait()

    table[...] = dot(gl[...], wg[...]).astype(BF16)

    for i in range(4, 8):
        loads[i].wait()
    pl.semaphore_wait(barrier, 3 + (NX - 1) + (NZ - 1) + 2 * (NY - 1) + jnp.where(moved, 2, 0))
    east_copy(0, ml).start()
    east_copy(1, ct).start()

    def gather(i, carry):
        rows = pl.ds(pl.multiple_of(i * 1024, 1024), 1024)
        pre[rows, :] = dot(pick[rows, :GRID_ROWS], table[...])
        return carry

    lax.fori_loop(0, SLOTS // 1024, gather, 0)

    def turn(i, carry):
        rows = pl.ds(pl.multiple_of(i * 256, 256), 256)
        glt[:, rows] = gl[rows, :].T
        return carry

    lax.fori_loop(0, GRID_ROWS // 256, turn, 0)

    east_copy(0, ml).wait_recv()
    east_copy(1, ct).wait_recv()
    mlt[...] = ml[...].T
    mtable[:, :D] = dot(ml[...], wm[...]).astype(BF16)
    mtable[:, D:] = dot_bt(ct[...], wo[...]).astype(BF16)

    def edge(i, carry):
        rows = pl.ds(pl.multiple_of(i * 1024, 1024), 1024)
        both = dot(pick[rows, GRID_ROWS:], mtable[...])
        value = pre[rows, :] + both[:, :D]
        sig = 0.5 * jnp.tanh(0.5 * value) + 0.5
        act = value * sig
        actgp[rows, :D] = act.astype(BF16)
        actgp[rows, D:] = (both[:, D:] * (sig + act * (1.0 - sig))).astype(BF16)
        return carry

    lax.fori_loop(0, SLOTS // 1024, edge, 0)

    def put(t, values):
        values = values.astype(BF16)
        for cc in range(NC):
            for xx in range(NX):
                for j in range(4):
                    first = block_row(t, cc, xx, j)
                    piece[t, cc, xx, 16 * j:16 * (j + 1)] = values[first:first + 16]
        core_copy(t).start()

    def after_core(t):
        core_copy(t).wait_recv()
        for xx in range(NX):
            total = piece[t, c, xx].astype(F32) + core_in[t, xx].astype(F32)
            mid[t, xx] = total.astype(BF16)
        for d in (2, 1, 3):
            x_copy(t, d).start()

    def after_x(t):
        for d in range(1, NX):
            x_copy(t, d).wait_recv()
        total = mid[t, x].astype(F32)
        for d in range(1, NX):
            total = total + x_in[t, d - 1].astype(F32)
        total = total.astype(BF16)
        for j in range(4):
            low[spot_z(x, t, j)] = total[16 * j:16 * (j + 1)]
        for j in range(4):
            @pl.when(z != spot_z(x, t, j))
            def _():
                z_copy(spot_z(x, t, j)).start()

    sums = dot(pickt[GRID_ROWS:, :], actgp[...])
    mine[...] = sums[:MESH_ROWS, D:]
    terms = sums[:, D:].astype(BF16)
    tosend[...] = terms[MESH_ROWS:]
    west_copy().start()
    put(OUT_TYPE, dot(sums[:, :D].T.astype(BF16), ct[...]))
    put(MESH_TYPE, dot(mlt[...], terms))

    def grid_side(first):
        def step(i, carry):
            rows = pl.ds(pl.multiple_of(i * 512, 512), 512)
            gpg[rows, :] = dot(pickt[rows, :], actgp[:, D:]).astype(BF16)
            return carry

        lax.fori_loop(first, first + 1, step, 0)

    grid_side(0)
    after_core(OUT_TYPE)
    after_core(MESH_TYPE)
    grid_side(1)
    put(GRID_TYPE, dot(glt[...], gpg[...]))

    def grid_grads(first):
        def step(i, carry):
            rows = pl.ds(pl.multiple_of(i * 512, 512), 512)
            gg[rows, :] = dot_bt(gpg[rows, :], wg[...]).astype(BF16)
            return carry

        lax.fori_loop(first, first + 1, step, 0)

    def store(i, source, goal):
        return pltpu.make_async_copy(source, goal, store_sem.at[i])

    grid_grads(0)
    after_core(GRID_TYPE)
    after_x(OUT_TYPE)
    after_x(MESH_TYPE)
    grid_grads(1)
    store(0, gg, gg_hbm).start()
    west_copy().wait_recv()
    mg[...] = dot_bt((mine[...] + west[...].astype(F32)).astype(BF16), wm[...]).astype(BF16)
    store(1, mg, mg_hbm).start()
    after_x(GRID_TYPE)

    whole(z_in, z_send, z_recv).wait_recv()
    total = low[z].astype(F32)
    for s in range(NZ - 1):
        total = total + z_in[s].astype(F32)
    last[...] = total.astype(BF16)

    for d in (4, 3, 5, 2, 6, 1, 7):
        y_copy((band + d) % NY, 0).start()

    @pl.when(moved)
    def _():
        y_copy(band, 1).start()

    @pl.when(jnp.logical_not(moved))
    def _():
        y_in[band] = last[...]

    rest = y_in.at[pl.ds(1, NY - 1)]
    whole(rest, y_send.at[0], y_recv.at[0]).wait_recv()

    @pl.when(moved)
    def _():
        y_copy(band, 1).wait_recv()

    total = y_in[0].astype(F32)
    for s in range(1, NY):
        total = total + y_in[s].astype(F32)
    wout[...] = total
    store(2, wout, wgrad_hbm).start()

    east_copy(0, ml).wait_send()
    east_copy(1, ct).wait_send()
    west_copy().wait_send()
    for t in range(3):
        core_copy(t).wait_send()
        for d in range(1, NX):
            x_copy(t, d).wait_send()
    whole(z_in, z_send, z_recv).wait_send()
    whole(rest, y_send.at[0], y_recv.at[0]).wait_send()

    @pl.when(moved)
    def _():
        y_copy(band, 1).wait_send()

    store(0, gg, gg_hbm).wait()
    store(1, mg, mg_hbm).wait()
    store(2, wout, wgrad_hbm).wait()


def hand_over(a, b, c, a_out, b_out, c_out, a_held, b_held, c_held, in_sem, out_sem):
    quarter = GRID_ROWS // 4
    parts = [(a.at[pl.ds(i * quarter, quarter)], a_held.at[pl.ds(i * quarter, quarter)],
              a_out.at[pl.ds(i * quarter, quarter)]) for i in range(4)]
    parts += [(b, b_held, b_out), (c, c_held, c_out)]
    reads = [pltpu.make_async_copy(source, held, in_sem.at[i]) for i, (source, held, _) in enumerate(parts)]
    writes = [pltpu.make_async_copy(held, goal, out_sem.at[i]) for i, (_, held, goal) in enumerate(parts)]
    for copy in reads:
        copy.start()
    for read, write in zip(reads, writes):
        read.wait()
        write.start()
    for copy in writes:
        copy.wait()


def on_device(
    grid_latent, mesh_latent, mesh_cotangent, w_grid, w_mesh, w_out, edge_source, edge_target, edge_count
):
    edges = (SLOTS // LANES, LANES)
    dma = pltpu.SemaphoreType.DMA
    vmem = pltpu.VMEM
    anywhere = pl.BlockSpec(memory_space=pl.ANY)
    results = (
        jax.ShapeDtypeStruct((GRID_ROWS, D), BF16),
        jax.ShapeDtypeStruct((MESH_ROWS, D), BF16),
        jax.ShapeDtypeStruct((16, D), F32),
    )
    made = pl.pallas_call(
        kernel,
        out_shape=results,
        in_specs=[anywhere] * 8 + [pl.BlockSpec(memory_space=pltpu.SMEM)],
        out_specs=[anywhere] * 3,
        scratch_shapes=[
            vmem((GRID_ROWS, D), BF16),
            vmem((D, GRID_ROWS), BF16),
            vmem((D, D), BF16),
            vmem((D, D), BF16),
            vmem((D, D), BF16),
            vmem((TABLE, D), BF16),
            vmem((D, TABLE), BF16),
            vmem((TABLE, D), BF16),
            vmem(edges, jnp.int32),
            vmem(edges, jnp.int32),
            vmem((SLOTS, GRID_ROWS + TABLE), BF16),
            vmem((GRID_ROWS + TABLE, SLOTS), BF16),
            vmem((GRID_ROWS, D), BF16),
            vmem((TABLE, 2 * D), BF16),
            vmem((SLOTS, D), F32),
            vmem((SLOTS, 2 * D), BF16),
            vmem((GRID_ROWS, D), BF16),
            vmem((GRID_ROWS, D), BF16),
            vmem((MESH_ROWS, D), BF16),
            vmem((MESH_ROWS, D), F32),
            vmem((MESH_ROWS, D), BF16),
            vmem((MESH_ROWS, D), BF16),
            vmem((3, NC, NX, 64, D), BF16),
            vmem((3, NX, 64, D), BF16),
            vmem((3, NX, 64, D), BF16),
            vmem((3, NX - 1, 64, D), BF16),
            vmem((NZ, 16, D), BF16),
            vmem((NZ - 1, 16, D), BF16),
            vmem((16, D), BF16),
            vmem((NY, 16, D), BF16),
            vmem((16, D), F32),
            dma((8,)),
            dma((3,)),
            dma((2,)),
            dma((2,)),
            dma,
            dma,
            dma((3,)),
            dma((3,)),
            dma((3, NX - 1)),
            dma((3, NX - 1)),
            dma,
            dma,
            dma((2,)),
            dma((2,)),
        ],
        compiler_params=pltpu.CompilerParams(
            collective_id=0, has_side_effects=True, vmem_limit_bytes=56 * 1024 * 1024
        ),
        cost_estimate=pl.CostEstimate(flops=17_000_000_000, bytes_accessed=5_000_000, transcendentals=1_000_000),
    )(
        grid_latent, mesh_latent, mesh_cotangent, w_grid, w_mesh, w_out,
        edge_source.reshape(edges), edge_target.reshape(edges), edge_count,
    )
    return pl.pallas_call(
        hand_over,
        out_shape=results,
        in_specs=[anywhere] * 3,
        out_specs=[anywhere] * 3,
        scratch_shapes=[
            vmem((GRID_ROWS, D), BF16), vmem((MESH_ROWS, D), BF16), vmem((16, D), F32), dma((6,)), dma((6,)),
        ],
        cost_estimate=pl.CostEstimate(flops=0, bytes_accessed=2_400_000, transcendentals=0),
    )(*made)


def solution(mesh):
    in_specs = (
        P(("band", "lon"), None),
        P(("band", "lon"), None),
        P(("band", "lon"), None),
        P(),
        P(),
        P(),
        P(("band", "lon")),
        P(("band", "lon")),
        P(("band", "lon")),
    )
    out_specs = (P(("band", "lon"), None), P(("band", "lon"), None), P("lon", None))
    return jax.shard_map(
        on_device, mesh=mesh, in_specs=in_specs, out_specs=out_specs, check_vma=False
    )
```

```python
import jax
import jax.numpy as jnp
from jax import lax
from jax.experimental import pallas as pl
from jax.experimental.pallas import tpu as pltpu
from jax.sharding import PartitionSpec as P

MESH = pl.DeviceIdType.MESH
BF16 = jnp.bfloat16
F32 = jnp.float32

D = 512
HALF = 256
GRID_ROWS = 1024
MESH_ROWS = 128
TABLE = 2 * MESH_ROWS
SLOTS = 2048
LANES = 128
NX, NY, NZ, NC = 4, 8, 12, 2
N_LON = NX * NZ * NC
GRID_TYPE, MESH_TYPE, OUT_TYPE = 0, 1, 2
SPOTS = (
    ((0, 0), (0, 1), (0, 2), (1, 0)),
    ((1, 1), (1, 2), (2, 0), (2, 1)),
    ((2, 2), (3, 0), (3, 1), (3, 2)),
)


def dot(a, b):
    return lax.dot_general(a, b, (((1,), (0,)), ((), ())), preferred_element_type=F32)


def dot_bt(a, b):
    return lax.dot_general(a, b, (((1,), (1,)), ((), ())), preferred_element_type=F32)


def lon_of(x, z, c):
    return (x * NZ + z) * NC + c


def spot_z(x, t, j):
    owner_x, group = SPOTS[t][j]
    return 4 * group + (x + NX - owner_x) % NX


def block_row(t, c, x, j):
    return 16 * (lon_of(SPOTS[t][j][0], spot_z(x, t, j), c) - 32 * t)


def kernel(
    gl_hbm, ml_hbm, ct_hbm, wg_hbm, wm_hbm, wo_hbm, src_hbm, tgt_hbm, cnt,
    gg_hbm, mg_hbm, wgrad_hbm,
    gl, glt, wg, wm, wo, ml, mlt, ct, src, tgt,
    pick, pickt, table, mtable, pre, actgp, gpg, gg, mg,
    mine, tosend, west,
    piece, core_in, mid, relay_in, x_in, grid_in, low, z_in, last, y_in, wout,
    load_sem, store_sem,
    east_send, east_recv, west_send, west_recv,
    core_send, core_recv, relay_send, relay_recv, x_send, x_recv, grid_send, grid_recv,
    z_send, z_recv, y_send, y_recv,
):
    band = lax.axis_index("band")
    lon = lax.axis_index("lon")
    x = lon // (NZ * NC)
    z = (lon // NC) % NZ
    c = lon % NC
    moved = z % NX != 0
    owner = lon_of((x + NZ - z) % NX, z, c)
    summer = lon_of((x + z) % NX, z, c)
    to_west = (band, (lon + N_LON - 1) % N_LON)
    to_east = (band, (lon + 1) % N_LON)
    mate = (band, lon_of(x, z, 1 - c))

    def load(i, source, target):
        return pltpu.make_async_copy(source, target, load_sem.at[i])

    loads = [
        load(0, src_hbm, src),
        load(1, tgt_hbm, tgt),
        load(2, gl_hbm, gl),
        load(3, wg_hbm, wg),
        load(4, ml_hbm, ml.at[pl.ds(0, MESH_ROWS)]),
        load(5, ct_hbm, ct.at[pl.ds(0, MESH_ROWS)]),
        load(6, wm_hbm, wm),
        load(7, wo_hbm, wo),
    ]
    for copy in loads:
        copy.start()

    barrier = pltpu.get_barrier_semaphore()

    def greet(device):
        pl.semaphore_signal(barrier, inc=1, device_id=device, device_id_type=MESH)

    greet(to_west)
    greet(to_east)
    greet(mate)
    for d in range(1, NX):
        greet((band, lon_of((x + d) % NX, z, c)))

    def greet_z(d, carry):
        greet((band, lon_of(x, (z + d) % NZ, c)))
        return carry

    lax.fori_loop(1, NZ, greet_z, 0)

    def greet_y(d, carry):
        greet(((band + d) % NY, owner))
        greet(((band + d) % NY, summer))
        return carry

    lax.fori_loop(1, NY, greet_y, 0)

    @pl.when(moved)
    def _():
        greet((band, owner))
        greet((band, summer))

    def east_copy(i, ref):
        return pltpu.make_async_remote_copy(
            src_ref=ref.at[pl.ds(0, MESH_ROWS)],
            dst_ref=ref.at[pl.ds(MESH_ROWS, MESH_ROWS)],
            send_sem=east_send.at[i],
            recv_sem=east_recv.at[i],
            device_id=to_west,
            device_id_type=MESH,
        )

    def west_copy():
        return pltpu.make_async_remote_copy(
            src_ref=tosend,
            dst_ref=west,
            send_sem=west_send,
            recv_sem=west_recv,
            device_id=to_east,
            device_id_type=MESH,
        )

    def core_copy(t):
        return pltpu.make_async_remote_copy(
            src_ref=piece.at[t, 1 - c],
            dst_ref=core_in.at[t],
            send_sem=core_send.at[t, 0],
            recv_sem=core_recv.at[t, 0],
            device_id=mate,
            device_id_type=MESH,
        )

    def core_half(h):
        return pltpu.make_async_remote_copy(
            src_ref=piece.at[GRID_TYPE, 1 - c, h],
            dst_ref=core_in.at[GRID_TYPE, h],
            send_sem=core_send.at[GRID_TYPE, h],
            recv_sem=core_recv.at[GRID_TYPE, h],
            device_id=mate,
            device_id_type=MESH,
        )

    next_x = (x + 1) % NX
    far_x = (x + 2) % NX
    prev_x = (x + 3) % NX

    def relay_copy(t, h):
        return pltpu.make_async_remote_copy(
            src_ref=mid.at[t, far_x, h],
            dst_ref=relay_in.at[t - 1, h],
            send_sem=relay_send.at[t - 1, h],
            recv_sem=relay_recv.at[t - 1, h],
            device_id=(band, lon_of(prev_x if h else next_x, z, c)),
            device_id_type=MESH,
        )

    def x_copy(t, way):
        there = prev_x if way else next_x
        return pltpu.make_async_remote_copy(
            src_ref=mid.at[t, there],
            dst_ref=x_in.at[t - 1, way],
            send_sem=x_send.at[t - 1, way],
            recv_sem=x_recv.at[t - 1, way],
            device_id=(band, lon_of(there, z, c)),
            device_id_type=MESH,
        )

    def grid_copy(h, d):
        there = (x + d) % NX
        return pltpu.make_async_remote_copy(
            src_ref=mid.at[GRID_TYPE, there, h],
            dst_ref=grid_in.at[h, d - 1],
            send_sem=grid_send.at[h, d - 1],
            recv_sem=grid_recv.at[h, d - 1],
            device_id=(band, lon_of(there, z, c)),
            device_id_type=MESH,
        )

    def z_copy(h, there):
        slot = (there + NZ - z + NZ - 1) % NZ
        return pltpu.make_async_remote_copy(
            src_ref=low.at[h, there],
            dst_ref=z_in.at[h, slot],
            send_sem=z_send.at[h],
            recv_sem=z_recv.at[h],
            device_id=(band, lon_of(x, there, c)),
            device_id_type=MESH,
        )

    def y_copy(h, y, i):
        return pltpu.make_async_remote_copy(
            src_ref=last.at[h],
            dst_ref=y_in.at[h, band],
            send_sem=y_send.at[h, i],
            recv_sem=y_recv.at[h, i],
            device_id=(y, owner),
            device_id_type=MESH,
        )

    def whole(ref, send, recv):
        return pltpu.make_async_remote_copy(
            src_ref=ref, dst_ref=ref, send_sem=send, recv_sem=recv,
            device_id=mate, device_id_type=MESH,
        )

    loads[0].wait()
    loads[1].wait()
    slot = lax.broadcasted_iota(jnp.int32, (SLOTS // LANES, LANES), 0) * LANES
    slot = slot + lax.broadcasted_iota(jnp.int32, (SLOTS // LANES, LANES), 1)
    target = tgt[...]
    start = (band * N_LON + lon) * MESH_ROWS
    here = (target >= start) & (target < start + MESH_ROWS)
    row = jnp.where(here, target - start, MESH_ROWS + (target & (MESH_ROWS - 1)))
    tgt[...] = jnp.where(slot < cnt[0], row + GRID_ROWS, -1)

    def build(r, carry):
        columns = pl.ds(pl.multiple_of(r * LANES, LANES), LANES)
        down = lax.broadcasted_iota(jnp.int32, (LANES, LANES), 0).astype(jnp.int16)
        across = lax.broadcasted_iota(jnp.int32, (LANES, LANES), 1).astype(jnp.int16)
        sb = jnp.broadcast_to(src[pl.ds(r, 1), :], (LANES, LANES)).astype(jnp.int16)
        tb = jnp.broadcast_to(tgt[pl.ds(r, 1), :], (LANES, LANES)).astype(jnp.int16)
        st = sb.T
        tt = tb.T
        for k in range((GRID_ROWS + TABLE) // LANES):
            one = (sb if k < GRID_ROWS // LANES else tb) == down + jnp.int16(k * LANES)
            pickt[k * LANES:(k + 1) * LANES, columns] = jnp.where(one, jnp.ones((), BF16), jnp.zeros((), BF16))
            one = (st if k < GRID_ROWS // LANES else tt) == across + jnp.int16(k * LANES)
            pick[columns, k * LANES:(k + 1) * LANES] = jnp.where(one, jnp.ones((), BF16), jnp.zeros((), BF16))
        return carry

    lax.fori_loop(0, SLOTS // LANES, build, 0)

    loads[2].wait()
    loads[3].wait()

    table[...] = dot(gl[...], wg[...]).astype(BF16)

    for i in range(4, 8):
        loads[i].wait()
    pl.semaphore_wait(barrier, 3 + (NX - 1) + (NZ - 1) + 2 * (NY - 1) + jnp.where(moved, 2, 0))
    east_copy(0, ml).start()
    east_copy(1, ct).start()

    def gather(i, carry):
        rows = pl.ds(pl.multiple_of(i * 1024, 1024), 1024)
        pre[rows, :] = dot(pick[rows, :GRID_ROWS], table[...])
        return carry

    lax.fori_loop(0, SLOTS // 1024, gather, 0)

    def turn(i, carry):
        rows = pl.ds(pl.multiple_of(i * 256, 256), 256)
        glt[:, rows] = gl[rows, :].T
        return carry

    lax.fori_loop(0, GRID_ROWS // 256, turn, 0)

    east_copy(0, ml).wait_recv()
    east_copy(1, ct).wait_recv()
    mlt[...] = ml[...].T
    mtable[:, :D] = dot(ml[...], wm[...]).astype(BF16)
    mtable[:, D:] = dot_bt(ct[...], wo[...]).astype(BF16)

    def edge(i, carry):
        rows = pl.ds(pl.multiple_of(i * 1024, 1024), 1024)
        both = dot(pick[rows, GRID_ROWS:], mtable[...])
        value = pre[rows, :] + both[:, :D]
        sig = 0.5 * jnp.tanh(0.5 * value) + 0.5
        act = value * sig
        actgp[rows, :D] = act.astype(BF16)
        actgp[rows, D:] = (both[:, D:] * (sig + act * (1.0 - sig))).astype(BF16)
        return carry

    lax.fori_loop(0, SLOTS // 1024, edge, 0)

    def put(t, h, values):
        values = values.astype(BF16)
        for cc in range(NC):
            for xx in range(NX):
                for j in range(4):
                    first = block_row(t, cc, xx, j)
                    piece[t, cc, h, xx, 16 * j:16 * (j + 1)] = values[first:first + 16]

    def after_core(t, h):
        for xx in range(NX):
            total = piece[t, c, h, xx].astype(F32) + core_in[t, h, xx].astype(F32)
            mid[t, xx, h] = total.astype(BF16)

    def to_z(t, h, total):
        total = total.astype(BF16)
        for j in range(4):
            low[h, spot_z(x, t, j)] = total[16 * j:16 * (j + 1)]
        for j in range(4):
            @pl.when(z != spot_z(x, t, j))
            def _():
                z_copy(h, spot_z(x, t, j)).start()

    def start_ring(t):
        core_copy(t).wait_recv()
        for h in range(2):
            after_core(t, h)
        for h in range(2):
            relay_copy(t, h).start()

    def step_ring(t):
        for h in range(2):
            relay_copy(t, h).wait_recv()
            there = prev_x if h else next_x
            total = mid[t, there, h].astype(F32) + relay_in[t - 1, h].astype(F32)
            mid[t, there, h] = total.astype(BF16)
        for way in range(2):
            x_copy(t, way).start()

    def end_ring(t):
        for way in range(2):
            x_copy(t, way).wait_recv()
        for h in range(2):
            total = mid[t, x, h].astype(F32) + x_in[t - 1, 0, h].astype(F32)
            to_z(t, h, total + x_in[t - 1, 1, h].astype(F32))

    def start_grid(h):
        core_half(h).wait_recv()
        after_core(GRID_TYPE, h)
        for d in (2, 1, 3):
            grid_copy(h, d).start()

    def end_grid(h):
        for d in range(1, NX):
            grid_copy(h, d).wait_recv()
        total = mid[GRID_TYPE, x, h].astype(F32)
        for d in range(1, NX):
            total = total + grid_in[h, d - 1].astype(F32)
        to_z(GRID_TYPE, h, total)

    sums = dot(pickt[GRID_ROWS:, :], actgp[...])
    mine[...] = sums[:MESH_ROWS, D:]
    terms = sums[:, D:].astype(BF16)
    tosend[...] = terms[MESH_ROWS:]
    west_copy().start()
    acts = sums[:, :D].T.astype(BF16)
    for h in range(2):
        put(OUT_TYPE, h, dot(acts, ct[:, h * HALF:(h + 1) * HALF]))
    core_copy(OUT_TYPE).start()
    for h in range(2):
        put(MESH_TYPE, h, dot(mlt[...], terms[:, h * HALF:(h + 1) * HALF]))
    core_copy(MESH_TYPE).start()

    def grid_side(first):
        def step(i, carry):
            rows = pl.ds(pl.multiple_of(i * 512, 512), 512)
            gpg[rows, :] = dot(pickt[rows, :], actgp[:, D:]).astype(BF16)
            return carry

        lax.fori_loop(first, first + 1, step, 0)

    grid_side(0)
    start_ring(OUT_TYPE)
    start_ring(MESH_TYPE)
    grid_side(1)
    for h in range(2):
        put(GRID_TYPE, h, dot(glt[...], gpg[:, h * HALF:(h + 1) * HALF]))
        core_half(h).start()

    def grid_grads(first):
        def step(i, carry):
            rows = pl.ds(pl.multiple_of(i * 512, 512), 512)
            gg[rows, :] = dot_bt(gpg[rows, :], wg[...]).astype(BF16)
            return carry

        lax.fori_loop(first, first + 1, step, 0)

    def store(i, source, goal):
        return pltpu.make_async_copy(source, goal, store_sem.at[i])

    step_ring(OUT_TYPE)
    step_ring(MESH_TYPE)
    start_grid(0)
    start_grid(1)
    grid_grads(0)
    end_ring(OUT_TYPE)
    end_ring(MESH_TYPE)
    grid_grads(1)
    store(0, gg, gg_hbm).start()
    west_copy().wait_recv()
    mg[...] = dot_bt((mine[...] + west[...].astype(F32)).astype(BF16), wm[...]).astype(BF16)
    store(1, mg, mg_hbm).start()
    end_grid(0)
    end_grid(1)

    for h in range(2):
        whole(z_in.at[h], z_send.at[h], z_recv.at[h]).wait_recv()
        total = low[h, z].astype(F32)
        for s in range(NZ - 1):
            total = total + z_in[h, s].astype(F32)
        last[h] = total.astype(BF16)
        for d in (4, 3, 5, 2, 6, 1, 7):
            y_copy(h, (band + d) % NY, 0).start()

        @pl.when(moved)
        def _():
            y_copy(h, band, 1).start()

        @pl.when(jnp.logical_not(moved))
        def _():
            y_in[h, band] = last[h]

    for h in range(2):
        rest = y_in.at[h, pl.ds(1, NY - 1)]
        whole(rest, y_send.at[h, 0], y_recv.at[h, 0]).wait_recv()

        @pl.when(moved)
        def _():
            y_copy(h, band, 1).wait_recv()

        total = y_in[h, 0].astype(F32)
        for s in range(1, NY):
            total = total + y_in[h, s].astype(F32)
        wout[:, h * HALF:(h + 1) * HALF] = total
    store(2, wout, wgrad_hbm).start()

    east_copy(0, ml).wait_send()
    east_copy(1, ct).wait_send()
    west_copy().wait_send()
    for t in (MESH_TYPE, OUT_TYPE):
        core_copy(t).wait_send()
        for h in range(2):
            relay_copy(t, h).wait_send()
            x_copy(t, h).wait_send()
    for h in range(2):
        core_half(h).wait_send()
        for d in range(1, NX):
            grid_copy(h, d).wait_send()
        whole(z_in.at[h], z_send.at[h], z_recv.at[h]).wait_send()
        whole(y_in.at[h, pl.ds(1, NY - 1)], y_send.at[h, 0], y_recv.at[h, 0]).wait_send()

        @pl.when(moved)
        def _():
            y_copy(h, band, 1).wait_send()

    store(0, gg, gg_hbm).wait()
    store(1, mg, mg_hbm).wait()
    store(2, wout, wgrad_hbm).wait()


def hand_over(a, b, c, a_out, b_out, c_out, a_held, b_held, c_held, in_sem, out_sem):
    quarter = GRID_ROWS // 4
    parts = [(a.at[pl.ds(i * quarter, quarter)], a_held.at[pl.ds(i * quarter, quarter)],
              a_out.at[pl.ds(i * quarter, quarter)]) for i in range(4)]
    parts += [(b, b_held, b_out), (c, c_held, c_out)]
    reads = [pltpu.make_async_copy(source, held, in_sem.at[i]) for i, (source, held, _) in enumerate(parts)]
    writes = [pltpu.make_async_copy(held, goal, out_sem.at[i]) for i, (_, held, goal) in enumerate(parts)]
    for copy in reads:
        copy.start()
    for read, write in zip(reads, writes):
        read.wait()
        write.start()
    for copy in writes:
        copy.wait()


def on_device(
    grid_latent, mesh_latent, mesh_cotangent, w_grid, w_mesh, w_out, edge_source, edge_target, edge_count
):
    edges = (SLOTS // LANES, LANES)
    dma = pltpu.SemaphoreType.DMA
    vmem = pltpu.VMEM
    anywhere = pl.BlockSpec(memory_space=pl.ANY)
    results = (
        jax.ShapeDtypeStruct((GRID_ROWS, D), BF16),
        jax.ShapeDtypeStruct((MESH_ROWS, D), BF16),
        jax.ShapeDtypeStruct((16, D), F32),
    )
    made = pl.pallas_call(
        kernel,
        out_shape=results,
        in_specs=[anywhere] * 8 + [pl.BlockSpec(memory_space=pltpu.SMEM)],
        out_specs=[anywhere] * 3,
        scratch_shapes=[
            vmem((GRID_ROWS, D), BF16),
            vmem((D, GRID_ROWS), BF16),
            vmem((D, D), BF16),
            vmem((D, D), BF16),
            vmem((D, D), BF16),
            vmem((TABLE, D), BF16),
            vmem((D, TABLE), BF16),
            vmem((TABLE, D), BF16),
            vmem(edges, jnp.int32),
            vmem(edges, jnp.int32),
            vmem((SLOTS, GRID_ROWS + TABLE), BF16),
            vmem((GRID_ROWS + TABLE, SLOTS), BF16),
            vmem((GRID_ROWS, D), BF16),
            vmem((TABLE, 2 * D), BF16),
            vmem((SLOTS, D), F32),
            vmem((SLOTS, 2 * D), BF16),
            vmem((GRID_ROWS, D), BF16),
            vmem((GRID_ROWS, D), BF16),
            vmem((MESH_ROWS, D), BF16),
            vmem((MESH_ROWS, D), F32),
            vmem((MESH_ROWS, D), BF16),
            vmem((MESH_ROWS, D), BF16),
            vmem((3, NC, 2, NX, 64, HALF), BF16),
            vmem((3, 2, NX, 64, HALF), BF16),
            vmem((3, NX, 2, 64, HALF), BF16),
            vmem((2, 2, 64, HALF), BF16),
            vmem((2, 2, 2, 64, HALF), BF16),
            vmem((2, NX - 1, 64, HALF), BF16),
            vmem((2, NZ, 16, HALF), BF16),
            vmem((2, NZ - 1, 16, HALF), BF16),
            vmem((2, 16, HALF), BF16),
            vmem((2, NY, 16, HALF), BF16),
            vmem((16, D), F32),
            dma((8,)),
            dma((3,)),
            dma((2,)),
            dma((2,)),
            dma,
            dma,
            dma((3, 2)),
            dma((3, 2)),
            dma((2, 2)),
            dma((2, 2)),
            dma((2, 2)),
            dma((2, 2)),
            dma((2, NX - 1)),
            dma((2, NX - 1)),
            dma((2,)),
            dma((2,)),
            dma((2, 2)),
            dma((2, 2)),
        ],
        compiler_params=pltpu.CompilerParams(
            collective_id=0, has_side_effects=True, vmem_limit_bytes=56 * 1024 * 1024
        ),
        cost_estimate=pl.CostEstimate(flops=17_000_000_000, bytes_accessed=5_000_000, transcendentals=1_000_000),
    )(
        grid_latent, mesh_latent, mesh_cotangent, w_grid, w_mesh, w_out,
        edge_source.reshape(edges), edge_target.reshape(edges), edge_count,
    )
    return pl.pallas_call(
        hand_over,
        out_shape=results,
        in_specs=[anywhere] * 3,
        out_specs=[anywhere] * 3,
        scratch_shapes=[
            vmem((GRID_ROWS, D), BF16), vmem((MESH_ROWS, D), BF16), vmem((16, D), F32), dma((6,)), dma((6,)),
        ],
        cost_estimate=pl.CostEstimate(flops=0, bytes_accessed=2_400_000, transcendentals=0),
    )(*made)


def solution(mesh):
    in_specs = (
        P(("band", "lon"), None),
        P(("band", "lon"), None),
        P(("band", "lon"), None),
        P(),
        P(),
        P(),
        P(("band", "lon")),
        P(("band", "lon")),
        P(("band", "lon")),
    )
    out_specs = (P(("band", "lon"), None), P(("band", "lon"), None), P("lon", None))
    return jax.shard_map(
        on_device, mesh=mesh, in_specs=in_specs, out_specs=out_specs, check_vma=False
    )
```

```python
import jax
import jax.numpy as jnp
from jax import lax
from jax.experimental import pallas as pl
from jax.experimental.pallas import tpu as pltpu
from jax.sharding import PartitionSpec as P

MESH = pl.DeviceIdType.MESH
BF16 = jnp.bfloat16
F32 = jnp.float32

D = 512
HALF = 256
GRID_ROWS = 1024
MESH_ROWS = 128
TABLE = 2 * MESH_ROWS
SLOTS = 2048
LANES = 128
NX, NY, NZ, NC = 4, 8, 12, 2
N_LON = NX * NZ * NC
ROUNDS = NZ // 2 - 1
GRID_TYPE, MESH_TYPE, OUT_TYPE = 0, 1, 2
SPOTS = (
    ((0, 0), (0, 1), (0, 2), (1, 0)),
    ((1, 1), (1, 2), (2, 0), (2, 1)),
    ((2, 2), (3, 0), (3, 1), (3, 2)),
)


def dot(a, b):
    return lax.dot_general(a, b, (((1,), (0,)), ((), ())), preferred_element_type=F32)


def dot_bt(a, b):
    return lax.dot_general(a, b, (((1,), (1,)), ((), ())), preferred_element_type=F32)


def lon_of(x, z, c):
    return (x * NZ + z) * NC + c


def spot_z(x, t, j):
    owner_x, group = SPOTS[t][j]
    return 4 * group + (x + NX - owner_x) % NX


def block_row(t, c, x, j):
    return 16 * (lon_of(SPOTS[t][j][0], spot_z(x, t, j), c) - 32 * t)


def kernel(
    gl_hbm, ml_hbm, ct_hbm, wg_hbm, wm_hbm, wo_hbm, src_hbm, tgt_hbm, cnt,
    gg_hbm, mg_hbm, wgrad_hbm,
    gl, glt, wg, wm, wo, ml, mlt, ct, src, tgt,
    pick, pickt, table, mtable, pre, actgp, gpg, gg, mg,
    mine, tosend, west,
    piece, core_in, mid, relay_in, x_in, grid_in, low, z_in, last, y_in, wout,
    load_sem, store_sem, token,
    east_send, east_recv, west_send, west_recv,
    core_send, core_recv, relay_send, relay_recv, x_send, x_recv, grid_send, grid_recv,
    z_send, z_recv, y_send, y_recv,
):
    band = lax.axis_index("band")
    lon = lax.axis_index("lon")
    x = lon // (NZ * NC)
    z = (lon // NC) % NZ
    c = lon % NC
    moved = z % NX != 0
    owner = lon_of((x + NZ - z) % NX, z, c)
    to_west = (band, (lon + N_LON - 1) % N_LON)
    to_east = (band, (lon + 1) % N_LON)
    mate = (band, lon_of(x, z, 1 - c))

    def load(i, source, target):
        return pltpu.make_async_copy(source, target, load_sem.at[i])

    loads = [
        load(0, ml_hbm, ml.at[pl.ds(0, MESH_ROWS)]),
        load(1, ct_hbm, ct.at[pl.ds(0, MESH_ROWS)]),
        load(2, src_hbm, src),
        load(3, tgt_hbm, tgt),
        load(4, gl_hbm, gl),
        load(5, wg_hbm, wg),
        load(6, wm_hbm, wm),
        load(7, wo_hbm, wo),
    ]
    for copy in loads:
        copy.start()

    barrier = pltpu.get_barrier_semaphore()

    def greet(device):
        pl.semaphore_signal(barrier, inc=1, device_id=device, device_id_type=MESH)

    greet(to_west)
    greet(to_east)
    greet(mate)
    for d in range(1, NX):
        greet((band, lon_of((x + d) % NX, z, c)))

    beside = [
        (band, lon_of(x, (z + 1) % NZ, c)),
        (band, lon_of(x, (z + NZ - 1) % NZ, c)),
        ((band + 1) % NY, lon),
        ((band + NY - 1) % NY, lon),
    ]
    for device in beside:
        greet(device)

    def tell(i):
        for device in beside:
            pl.semaphore_signal(token.at[i], inc=1, device_id=device, device_id_type=MESH)

    def hear(i):
        pl.semaphore_wait(token.at[i], len(beside))

    def east_copy(i, ref):
        return pltpu.make_async_remote_copy(
            src_ref=ref.at[pl.ds(0, MESH_ROWS)],
            dst_ref=ref.at[pl.ds(MESH_ROWS, MESH_ROWS)],
            send_sem=east_send.at[i],
            recv_sem=east_recv.at[i],
            device_id=to_west,
            device_id_type=MESH,
        )

    def west_copy():
        return pltpu.make_async_remote_copy(
            src_ref=tosend,
            dst_ref=west,
            send_sem=west_send,
            recv_sem=west_recv,
            device_id=to_east,
            device_id_type=MESH,
        )

    def core_copy(t):
        return pltpu.make_async_remote_copy(
            src_ref=piece.at[t, 1 - c],
            dst_ref=core_in.at[t],
            send_sem=core_send.at[t, 0],
            recv_sem=core_recv.at[t, 0],
            device_id=mate,
            device_id_type=MESH,
        )

    def core_half(h):
        return pltpu.make_async_remote_copy(
            src_ref=piece.at[GRID_TYPE, 1 - c, h],
            dst_ref=core_in.at[GRID_TYPE, h],
            send_sem=core_send.at[GRID_TYPE, h],
            recv_sem=core_recv.at[GRID_TYPE, h],
            device_id=mate,
            device_id_type=MESH,
        )

    next_x = (x + 1) % NX
    far_x = (x + 2) % NX
    prev_x = (x + 3) % NX

    def relay_copy(t, h):
        return pltpu.make_async_remote_copy(
            src_ref=mid.at[t, far_x, h],
            dst_ref=relay_in.at[t - 1, h],
            send_sem=relay_send.at[t - 1, h],
            recv_sem=relay_recv.at[t - 1, h],
            device_id=(band, lon_of(prev_x if h else next_x, z, c)),
            device_id_type=MESH,
        )

    def x_copy(t, way, h):
        there = prev_x if way else next_x
        return pltpu.make_async_remote_copy(
            src_ref=mid.at[t, there, h],
            dst_ref=x_in.at[t - 1, way, h],
            send_sem=x_send.at[t - 1, way, h],
            recv_sem=x_recv.at[t - 1, way, h],
            device_id=(band, lon_of(there, z, c)),
            device_id_type=MESH,
        )

    def grid_copy(h, d):
        there = (x + d) % NX
        return pltpu.make_async_remote_copy(
            src_ref=mid.at[GRID_TYPE, there, h],
            dst_ref=grid_in.at[h, d - 1],
            send_sem=grid_send.at[h, d - 1],
            recv_sem=grid_recv.at[h, d - 1],
            device_id=(band, lon_of(there, z, c)),
            device_id_type=MESH,
        )

    def z_copy(h, there):
        slot = (there + NZ - z + NZ - 1) % NZ
        return pltpu.make_async_remote_copy(
            src_ref=low.at[h, there],
            dst_ref=z_in.at[h, slot],
            send_sem=z_send.at[h],
            recv_sem=z_recv.at[h],
            device_id=(band, lon_of(x, there, c)),
            device_id_type=MESH,
        )

    def y_copy(h, y, i):
        return pltpu.make_async_remote_copy(
            src_ref=last.at[h],
            dst_ref=y_in.at[h, band],
            send_sem=y_send.at[h, i],
            recv_sem=y_recv.at[h, i],
            device_id=(y, owner),
            device_id_type=MESH,
        )

    def whole(ref, send, recv):
        return pltpu.make_async_remote_copy(
            src_ref=ref, dst_ref=ref, send_sem=send, recv_sem=recv,
            device_id=mate, device_id_type=MESH,
        )

    loads[0].wait()
    loads[1].wait()
    pl.semaphore_wait(barrier, 3 + (NX - 1) + len(beside))
    east_copy(0, ml).start()
    east_copy(1, ct).start()
    tell(0)

    loads[2].wait()
    loads[3].wait()
    slot = lax.broadcasted_iota(jnp.int32, (SLOTS // LANES, LANES), 0) * LANES
    slot = slot + lax.broadcasted_iota(jnp.int32, (SLOTS // LANES, LANES), 1)
    target = tgt[...]
    start = (band * N_LON + lon) * MESH_ROWS
    here = (target >= start) & (target < start + MESH_ROWS)
    row = jnp.where(here, target - start, MESH_ROWS + (target & (MESH_ROWS - 1)))
    tgt[...] = jnp.where(slot < cnt[0], row + GRID_ROWS, -1)

    def build(r, carry):
        columns = pl.ds(pl.multiple_of(r * LANES, LANES), LANES)
        down = lax.broadcasted_iota(jnp.int32, (LANES, LANES), 0).astype(jnp.int16)
        across = lax.broadcasted_iota(jnp.int32, (LANES, LANES), 1).astype(jnp.int16)
        sb = jnp.broadcast_to(src[pl.ds(r, 1), :], (LANES, LANES)).astype(jnp.int16)
        tb = jnp.broadcast_to(tgt[pl.ds(r, 1), :], (LANES, LANES)).astype(jnp.int16)
        st = sb.T
        tt = tb.T
        for k in range((GRID_ROWS + TABLE) // LANES):
            one = (sb if k < GRID_ROWS // LANES else tb) == down + jnp.int16(k * LANES)
            pickt[k * LANES:(k + 1) * LANES, columns] = jnp.where(one, jnp.ones((), BF16), jnp.zeros((), BF16))
            one = (st if k < GRID_ROWS // LANES else tt) == across + jnp.int16(k * LANES)
            pick[columns, k * LANES:(k + 1) * LANES] = jnp.where(one, jnp.ones((), BF16), jnp.zeros((), BF16))
        return carry

    lax.fori_loop(0, SLOTS // LANES, build, 0)

    hear(0)
    tell(1)

    loads[4].wait()
    loads[5].wait()
    table[...] = dot(gl[...], wg[...]).astype(BF16)
    hear(1)
    tell(2)

    def gather(i, carry):
        rows = pl.ds(pl.multiple_of(i * 1024, 1024), 1024)
        pre[rows, :] = dot(pick[rows, :GRID_ROWS], table[...])
        return carry

    lax.fori_loop(0, SLOTS // 1024, gather, 0)
    hear(2)
    tell(3)

    def turn(i, carry):
        rows = pl.ds(pl.multiple_of(i * 256, 256), 256)
        glt[:, rows] = gl[rows, :].T
        return carry

    lax.fori_loop(0, GRID_ROWS // 256, turn, 0)

    loads[6].wait()
    loads[7].wait()
    east_copy(0, ml).wait_recv()
    east_copy(1, ct).wait_recv()
    mlt[...] = ml[...].T
    mtable[:, :D] = dot(ml[...], wm[...]).astype(BF16)
    mtable[:, D:] = dot_bt(ct[...], wo[...]).astype(BF16)

    def edge(i, carry):
        rows = pl.ds(pl.multiple_of(i * 1024, 1024), 1024)
        both = dot(pick[rows, GRID_ROWS:], mtable[...])
        value = pre[rows, :] + both[:, :D]
        sig = 0.5 * jnp.tanh(0.5 * value) + 0.5
        act = value * sig
        actgp[rows, :D] = act.astype(BF16)
        actgp[rows, D:] = (both[:, D:] * (sig + act * (1.0 - sig))).astype(BF16)
        return carry

    lax.fori_loop(0, SLOTS // 1024, edge, 0)
    hear(3)
    tell(4)

    def put(t, h, values):
        values = values.astype(BF16)
        for cc in range(NC):
            for xx in range(NX):
                for j in range(4):
                    first = block_row(t, cc, xx, j)
                    piece[t, cc, h, xx, 16 * j:16 * (j + 1)] = values[first:first + 16]

    def after_core(t, h):
        for xx in range(NX):
            total = piece[t, c, h, xx].astype(F32) + core_in[t, h, xx].astype(F32)
            mid[t, xx, h] = total.astype(BF16)

    def to_z(t, h, total):
        total = total.astype(BF16)
        for j in range(4):
            low[h, spot_z(x, t, j)] = total[16 * j:16 * (j + 1)]
        for j in range(4):
            @pl.when(z != spot_z(x, t, j))
            def _():
                z_copy(h, spot_z(x, t, j)).start()

    def start_ring(t):
        core_copy(t).wait_recv()
        for h in range(2):
            after_core(t, h)
        for h in range(2):
            relay_copy(t, h).start()
        for h in range(2):
            x_copy(t, 1 - h, h).start()

    def step_ring(t):
        for h in range(2):
            relay_copy(t, h).wait_recv()
            there = prev_x if h else next_x
            total = mid[t, there, h].astype(F32) + relay_in[t - 1, h].astype(F32)
            mid[t, there, h] = total.astype(BF16)
            x_copy(t, h, h).start()

    def end_ring(t):
        for h in range(2):
            x_copy(t, 0, h).wait_recv()
            x_copy(t, 1, h).wait_recv()
            total = mid[t, x, h].astype(F32) + x_in[t - 1, 0, h].astype(F32)
            to_z(t, h, total + x_in[t - 1, 1, h].astype(F32))

    def start_grid(h):
        core_half(h).wait_recv()
        after_core(GRID_TYPE, h)
        for d in (2, 1, 3):
            grid_copy(h, d).start()

    def end_grid(h):
        for d in range(1, NX):
            grid_copy(h, d).wait_recv()
        total = mid[GRID_TYPE, x, h].astype(F32)
        for d in range(1, NX):
            total = total + grid_in[h, d - 1].astype(F32)
        to_z(GRID_TYPE, h, total)

    sums = dot(pickt[GRID_ROWS:, :], actgp[...])
    mine[...] = sums[:MESH_ROWS, D:]
    terms = sums[:, D:].astype(BF16)
    tosend[...] = terms[MESH_ROWS:]
    west_copy().start()
    acts = sums[:, :D].T.astype(BF16)
    for h in range(2):
        put(OUT_TYPE, h, dot(acts, ct[:, h * HALF:(h + 1) * HALF]))
    core_copy(OUT_TYPE).start()
    for h in range(2):
        put(MESH_TYPE, h, dot(mlt[...], terms[:, h * HALF:(h + 1) * HALF]))
    core_copy(MESH_TYPE).start()

    def grid_side(first):
        def step(i, carry):
            rows = pl.ds(pl.multiple_of(i * 512, 512), 512)
            gpg[rows, :] = dot(pickt[rows, :], actgp[:, D:]).astype(BF16)
            return carry

        lax.fori_loop(first, first + 1, step, 0)

    grid_side(0)
    start_ring(OUT_TYPE)
    start_ring(MESH_TYPE)
    grid_side(1)
    for h in range(2):
        put(GRID_TYPE, h, dot(glt[...], gpg[:, h * HALF:(h + 1) * HALF]))
        core_half(h).start()

    def grid_grads(first):
        def step(i, carry):
            rows = pl.ds(pl.multiple_of(i * 512, 512), 512)
            gg[rows, :] = dot_bt(gpg[rows, :], wg[...]).astype(BF16)
            return carry

        lax.fori_loop(first, first + 1, step, 0)

    def store(i, source, goal):
        return pltpu.make_async_copy(source, goal, store_sem.at[i])

    step_ring(OUT_TYPE)
    step_ring(MESH_TYPE)
    start_grid(0)
    start_grid(1)
    grid_grads(0)
    hear(4)
    end_ring(OUT_TYPE)
    end_ring(MESH_TYPE)
    grid_grads(1)
    store(0, gg, gg_hbm).start()
    west_copy().wait_recv()
    mg[...] = dot_bt((mine[...] + west[...].astype(F32)).astype(BF16), wm[...]).astype(BF16)
    store(1, mg, mg_hbm).start()
    end_grid(0)
    end_grid(1)

    for h in range(2):
        whole(z_in.at[h], z_send.at[h], z_recv.at[h]).wait_recv()
        total = low[h, z].astype(F32)
        for s in range(NZ - 1):
            total = total + z_in[h, s].astype(F32)
        last[h] = total.astype(BF16)
        for d in (4, 3, 5, 2, 6, 1, 7):
            y_copy(h, (band + d) % NY, 0).start()

        @pl.when(moved)
        def _():
            y_copy(h, band, 1).start()

        @pl.when(jnp.logical_not(moved))
        def _():
            y_in[h, band] = last[h]

    for h in range(2):
        rest = y_in.at[h, pl.ds(1, NY - 1)]
        whole(rest, y_send.at[h, 0], y_recv.at[h, 0]).wait_recv()

        @pl.when(moved)
        def _():
            y_copy(h, band, 1).wait_recv()

        total = y_in[h, 0].astype(F32)
        for s in range(1, NY):
            total = total + y_in[h, s].astype(F32)
        wout[:, h * HALF:(h + 1) * HALF] = total
    store(2, wout, wgrad_hbm).start()

    east_copy(0, ml).wait_send()
    east_copy(1, ct).wait_send()
    west_copy().wait_send()
    for t in (MESH_TYPE, OUT_TYPE):
        core_copy(t).wait_send()
        for h in range(2):
            relay_copy(t, h).wait_send()
            x_copy(t, 0, h).wait_send()
            x_copy(t, 1, h).wait_send()
    for h in range(2):
        core_half(h).wait_send()
        for d in range(1, NX):
            grid_copy(h, d).wait_send()
        whole(z_in.at[h], z_send.at[h], z_recv.at[h]).wait_send()
        whole(y_in.at[h, pl.ds(1, NY - 1)], y_send.at[h, 0], y_recv.at[h, 0]).wait_send()

        @pl.when(moved)
        def _():
            y_copy(h, band, 1).wait_send()

    store(0, gg, gg_hbm).wait()
    store(1, mg, mg_hbm).wait()
    store(2, wout, wgrad_hbm).wait()


def hand_over(a, b, c, a_out, b_out, c_out, a_held, b_held, c_held, in_sem, out_sem):
    quarter = GRID_ROWS // 4
    parts = [(a.at[pl.ds(i * quarter, quarter)], a_held.at[pl.ds(i * quarter, quarter)],
              a_out.at[pl.ds(i * quarter, quarter)]) for i in range(4)]
    parts += [(b, b_held, b_out), (c, c_held, c_out)]
    reads = [pltpu.make_async_copy(source, held, in_sem.at[i]) for i, (source, held, _) in enumerate(parts)]
    writes = [pltpu.make_async_copy(held, goal, out_sem.at[i]) for i, (_, held, goal) in enumerate(parts)]
    for copy in reads:
        copy.start()
    for read, write in zip(reads, writes):
        read.wait()
        write.start()
    for copy in writes:
        copy.wait()


def on_device(
    grid_latent, mesh_latent, mesh_cotangent, w_grid, w_mesh, w_out, edge_source, edge_target, edge_count
):
    edges = (SLOTS // LANES, LANES)
    dma = pltpu.SemaphoreType.DMA
    vmem = pltpu.VMEM
    anywhere = pl.BlockSpec(memory_space=pl.ANY)
    results = (
        jax.ShapeDtypeStruct((GRID_ROWS, D), BF16),
        jax.ShapeDtypeStruct((MESH_ROWS, D), BF16),
        jax.ShapeDtypeStruct((16, D), F32),
    )
    made = pl.pallas_call(
        kernel,
        out_shape=results,
        in_specs=[anywhere] * 8 + [pl.BlockSpec(memory_space=pltpu.SMEM)],
        out_specs=[anywhere] * 3,
        scratch_shapes=[
            vmem((GRID_ROWS, D), BF16),
            vmem((D, GRID_ROWS), BF16),
            vmem((D, D), BF16),
            vmem((D, D), BF16),
            vmem((D, D), BF16),
            vmem((TABLE, D), BF16),
            vmem((D, TABLE), BF16),
            vmem((TABLE, D), BF16),
            vmem(edges, jnp.int32),
            vmem(edges, jnp.int32),
            vmem((SLOTS, GRID_ROWS + TABLE), BF16),
            vmem((GRID_ROWS + TABLE, SLOTS), BF16),
            vmem((GRID_ROWS, D), BF16),
            vmem((TABLE, 2 * D), BF16),
            vmem((SLOTS, D), F32),
            vmem((SLOTS, 2 * D), BF16),
            vmem((GRID_ROWS, D), BF16),
            vmem((GRID_ROWS, D), BF16),
            vmem((MESH_ROWS, D), BF16),
            vmem((MESH_ROWS, D), F32),
            vmem((MESH_ROWS, D), BF16),
            vmem((MESH_ROWS, D), BF16),
            vmem((3, NC, 2, NX, 64, HALF), BF16),
            vmem((3, 2, NX, 64, HALF), BF16),
            vmem((3, NX, 2, 64, HALF), BF16),
            vmem((2, 2, 64, HALF), BF16),
            vmem((2, 2, 2, 64, HALF), BF16),
            vmem((2, NX - 1, 64, HALF), BF16),
            vmem((2, NZ, 16, HALF), BF16),
            vmem((2, NZ - 1, 16, HALF), BF16),
            vmem((2, 16, HALF), BF16),
            vmem((2, NY, 16, HALF), BF16),
            vmem((16, D), F32),
            dma((8,)),
            dma((3,)),
            pltpu.SemaphoreType.REGULAR((ROUNDS,)),
            dma((2,)),
            dma((2,)),
            dma,
            dma,
            dma((3, 2)),
            dma((3, 2)),
            dma((2, 2)),
            dma((2, 2)),
            dma((2, 2, 2)),
            dma((2, 2, 2)),
            dma((2, NX - 1)),
            dma((2, NX - 1)),
            dma((2,)),
            dma((2,)),
            dma((2, 2)),
            dma((2, 2)),
        ],
        compiler_params=pltpu.CompilerParams(
            collective_id=0, has_side_effects=True, vmem_limit_bytes=56 * 1024 * 1024
        ),
        cost_estimate=pl.CostEstimate(flops=17_000_000_000, bytes_accessed=5_000_000, transcendentals=1_000_000),
    )(
        grid_latent, mesh_latent, mesh_cotangent, w_grid, w_mesh, w_out,
        edge_source.reshape(edges), edge_target.reshape(edges), edge_count,
    )
    return pl.pallas_call(
        hand_over,
        out_shape=results,
        in_specs=[anywhere] * 3,
        out_specs=[anywhere] * 3,
        scratch_shapes=[
            vmem((GRID_ROWS, D), BF16), vmem((MESH_ROWS, D), BF16), vmem((16, D), F32), dma((6,)), dma((6,)),
        ],
        cost_estimate=pl.CostEstimate(flops=0, bytes_accessed=2_400_000, transcendentals=0),
    )(*made)


def solution(mesh):
    in_specs = (
        P(("band", "lon"), None),
        P(("band", "lon"), None),
        P(("band", "lon"), None),
        P(),
        P(),
        P(),
        P(("band", "lon")),
        P(("band", "lon")),
        P(("band", "lon")),
    )
    out_specs = (P(("band", "lon"), None), P(("band", "lon"), None), P("lon", None))
    return jax.shard_map(
        on_device, mesh=mesh, in_specs=in_specs, out_specs=out_specs, check_vma=False
    )
```

```python
import jax
import jax.numpy as jnp
from jax import lax
from jax.experimental import pallas as pl
from jax.experimental.pallas import tpu as pltpu
from jax.sharding import PartitionSpec as P

MESH = pl.DeviceIdType.MESH
BF16 = jnp.bfloat16
F32 = jnp.float32

D = 512
HALF = 256
GRID_ROWS = 1024
MESH_ROWS = 128
TABLE = 2 * MESH_ROWS
SLOTS = 2048
LANES = 128
CHUNK = 512
NX, NY, NZ, NC = 4, 8, 12, 2
N_LON = NX * NZ * NC
ROUNDS = NZ // 2 - 1
GRID_TYPE, MESH_TYPE, OUT_TYPE = 0, 1, 2
SPOTS = (
    ((0, 0), (0, 1), (0, 2), (1, 0)),
    ((1, 1), (1, 2), (2, 0), (2, 1)),
    ((2, 2), (3, 0), (3, 1), (3, 2)),
)


def dot(a, b):
    return lax.dot_general(a, b, (((1,), (0,)), ((), ())), preferred_element_type=F32)


def dot_bt(a, b):
    return lax.dot_general(a, b, (((1,), (1,)), ((), ())), preferred_element_type=F32)


def lon_of(x, z, c):
    return (x * NZ + z) * NC + c


def spot_z(x, t, j):
    owner_x, group = SPOTS[t][j]
    return 4 * group + (x + NX - owner_x) % NX


def block_row(t, c, x, j):
    return 16 * (lon_of(SPOTS[t][j][0], spot_z(x, t, j), c) - 32 * t)


def kernel(
    gl_hbm, ml_hbm, ct_hbm, wg_hbm, wm_hbm, wo_hbm, src_hbm, tgt_hbm, cnt,
    gg_hbm, mg_hbm, wgrad_hbm,
    gl, glt, wg, wm, wo, ml, mlt, ct, src, tgt,
    pick, pickt, table, mtable, pre, actgp, gpg, gg, mg,
    mine, tosend, west,
    piece, core_in, mid, relay_in, x_in, grid_in, low, z_in, last, y_in, wout,
    load_sem, store_sem, token,
    east_send, east_recv, west_send, west_recv,
    core_send, core_recv, relay_send, relay_recv, x_send, x_recv, grid_send, grid_recv,
    z_send, z_recv, y_send, y_recv,
):
    band = lax.axis_index("band")
    lon = lax.axis_index("lon")
    x = lon // (NZ * NC)
    z = (lon // NC) % NZ
    c = lon % NC
    moved = z % NX != 0
    owner = lon_of((x + NZ - z) % NX, z, c)
    to_west = (band, (lon + N_LON - 1) % N_LON)
    to_east = (band, (lon + 1) % N_LON)
    mate = (band, lon_of(x, z, 1 - c))

    def load(i, source, target):
        return pltpu.make_async_copy(source, target, load_sem.at[i])

    loads = [
        load(0, ml_hbm, ml.at[pl.ds(0, MESH_ROWS)]),
        load(1, ct_hbm, ct.at[pl.ds(0, MESH_ROWS)]),
        load(2, src_hbm, src),
        load(3, tgt_hbm, tgt),
        load(4, gl_hbm, gl),
        load(5, wg_hbm, wg),
        load(6, wm_hbm, wm),
        load(7, wo_hbm, wo),
    ]
    for copy in loads:
        copy.start()

    barrier = pltpu.get_barrier_semaphore()

    def greet(device):
        pl.semaphore_signal(barrier, inc=1, device_id=device, device_id_type=MESH)

    greet(to_west)
    greet(to_east)
    greet(mate)
    for d in range(1, NX):
        greet((band, lon_of((x + d) % NX, z, c)))

    beside = [
        (band, lon_of(x, (z + 1) % NZ, c)),
        (band, lon_of(x, (z + NZ - 1) % NZ, c)),
        ((band + 1) % NY, lon),
        ((band + NY - 1) % NY, lon),
    ]
    for device in beside:
        greet(device)

    def tell(i):
        for device in beside:
            pl.semaphore_signal(token.at[i], inc=1, device_id=device, device_id_type=MESH)

    def hear(i):
        pl.semaphore_wait(token.at[i], len(beside))

    def east_copy(i, ref):
        return pltpu.make_async_remote_copy(
            src_ref=ref.at[pl.ds(0, MESH_ROWS)],
            dst_ref=ref.at[pl.ds(MESH_ROWS, MESH_ROWS)],
            send_sem=east_send.at[i],
            recv_sem=east_recv.at[i],
            device_id=to_west,
            device_id_type=MESH,
        )

    def west_copy():
        return pltpu.make_async_remote_copy(
            src_ref=tosend,
            dst_ref=west,
            send_sem=west_send,
            recv_sem=west_recv,
            device_id=to_east,
            device_id_type=MESH,
        )

    def core_copy(t):
        return pltpu.make_async_remote_copy(
            src_ref=piece.at[t, 1 - c],
            dst_ref=core_in.at[t],
            send_sem=core_send.at[t, 0],
            recv_sem=core_recv.at[t, 0],
            device_id=mate,
            device_id_type=MESH,
        )

    def core_half(h):
        return pltpu.make_async_remote_copy(
            src_ref=piece.at[GRID_TYPE, 1 - c, h],
            dst_ref=core_in.at[GRID_TYPE, h],
            send_sem=core_send.at[GRID_TYPE, h],
            recv_sem=core_recv.at[GRID_TYPE, h],
            device_id=mate,
            device_id_type=MESH,
        )

    next_x = (x + 1) % NX
    far_x = (x + 2) % NX
    prev_x = (x + 3) % NX

    def relay_copy(t, h):
        return pltpu.make_async_remote_copy(
            src_ref=mid.at[t, far_x, h],
            dst_ref=relay_in.at[t - 1, h],
            send_sem=relay_send.at[t - 1, h],
            recv_sem=relay_recv.at[t - 1, h],
            device_id=(band, lon_of(prev_x if h else next_x, z, c)),
            device_id_type=MESH,
        )

    def x_copy(t, way, h):
        there = prev_x if way else next_x
        return pltpu.make_async_remote_copy(
            src_ref=mid.at[t, there, h],
            dst_ref=x_in.at[t - 1, way, h],
            send_sem=x_send.at[t - 1, way, h],
            recv_sem=x_recv.at[t - 1, way, h],
            device_id=(band, lon_of(there, z, c)),
            device_id_type=MESH,
        )

    def grid_copy(h, d):
        there = (x + d) % NX
        return pltpu.make_async_remote_copy(
            src_ref=mid.at[GRID_TYPE, there, h],
            dst_ref=grid_in.at[h, d - 1],
            send_sem=grid_send.at[h, d - 1],
            recv_sem=grid_recv.at[h, d - 1],
            device_id=(band, lon_of(there, z, c)),
            device_id_type=MESH,
        )

    def z_copy(h, there):
        slot = (there + NZ - z + NZ - 1) % NZ
        return pltpu.make_async_remote_copy(
            src_ref=low.at[h, there],
            dst_ref=z_in.at[h, slot],
            send_sem=z_send.at[h],
            recv_sem=z_recv.at[h],
            device_id=(band, lon_of(x, there, c)),
            device_id_type=MESH,
        )

    def y_copy(h, y, i):
        return pltpu.make_async_remote_copy(
            src_ref=last.at[h],
            dst_ref=y_in.at[h, band],
            send_sem=y_send.at[h, i],
            recv_sem=y_recv.at[h, i],
            device_id=(y, owner),
            device_id_type=MESH,
        )

    def whole(ref, send, recv):
        return pltpu.make_async_remote_copy(
            src_ref=ref, dst_ref=ref, send_sem=send, recv_sem=recv,
            device_id=mate, device_id_type=MESH,
        )

    loads[0].wait()
    loads[1].wait()
    pl.semaphore_wait(barrier, 3 + (NX - 1) + len(beside))
    east_copy(0, ml).start()
    east_copy(1, ct).start()
    tell(0)

    loads[2].wait()
    loads[3].wait()
    slot = lax.broadcasted_iota(jnp.int32, (SLOTS // LANES, LANES), 0) * LANES
    slot = slot + lax.broadcasted_iota(jnp.int32, (SLOTS // LANES, LANES), 1)
    target = tgt[...]
    start = (band * N_LON + lon) * MESH_ROWS
    here = (target >= start) & (target < start + MESH_ROWS)
    row = jnp.where(here, target - start, MESH_ROWS + (target & (MESH_ROWS - 1)))
    tgt[...] = jnp.where(slot < cnt[0], row + GRID_ROWS, -1)

    across = lax.broadcasted_iota(jnp.int32, (LANES, LANES), 1).astype(jnp.int16)
    down = lax.broadcasted_iota(jnp.int32, (LANES, LANES), 0).astype(jnp.int16)

    def build(r):
        columns = slice(r * LANES, (r + 1) * LANES)
        sb = jnp.broadcast_to(src[r:r + 1, :], (LANES, LANES)).astype(jnp.int16)
        tb = jnp.broadcast_to(tgt[r:r + 1, :], (LANES, LANES)).astype(jnp.int16)
        st = sb.T
        tt = tb.T
        for k in range((GRID_ROWS + TABLE) // LANES):
            one = (sb if k < GRID_ROWS // LANES else tb) == down + jnp.int16(k * LANES)
            pickt[k * LANES:(k + 1) * LANES, columns] = jnp.where(one, jnp.ones((), BF16), jnp.zeros((), BF16))
            one = (st if k < GRID_ROWS // LANES else tt) == across + jnp.int16(k * LANES)
            pick[columns, k * LANES:(k + 1) * LANES] = jnp.where(one, jnp.ones((), BF16), jnp.zeros((), BF16))

    def build_chunk(i):
        for r in range(CHUNK // LANES):
            build(i * (CHUNK // LANES) + r)

    build_chunk(0)

    hear(0)
    tell(1)

    loads[4].wait()
    loads[5].wait()
    table[...] = dot(gl[...], wg[...]).astype(BF16)
    build_chunk(1)
    hear(1)
    tell(2)

    for first in range(0, SLOTS, CHUNK):
        pre[first:first + CHUNK, :] = dot(pick[first:first + CHUNK, :GRID_ROWS], table[...])
        if first + 2 * CHUNK < SLOTS:
            build_chunk(first // CHUNK + 2)
        else:
            turned = slice(GRID_ROWS * (first - SLOTS + 2 * CHUNK) // (2 * CHUNK), GRID_ROWS * (first - SLOTS + 3 * CHUNK) // (2 * CHUNK))
            glt[:, turned] = gl[turned, :].T
    hear(2)
    tell(3)


    loads[6].wait()
    loads[7].wait()
    east_copy(0, ml).wait_recv()
    east_copy(1, ct).wait_recv()
    mlt[...] = ml[...].T
    mtable[:, :D] = dot(ml[...], wm[...]).astype(BF16)
    mtable[:, D:] = dot_bt(ct[...], wo[...]).astype(BF16)

    for first in range(0, SLOTS, 512):
        rows = slice(first, first + 512)
        both = dot(pick[rows, GRID_ROWS:], mtable[...])
        value = pre[rows, :] + both[:, :D]
        sig = 0.5 * jnp.tanh(0.5 * value) + 0.5
        act = value * sig
        actgp[rows, :D] = act.astype(BF16)
        actgp[rows, D:] = (both[:, D:] * (sig + act * (1.0 - sig))).astype(BF16)

    hear(3)
    tell(4)

    def put(t, h, values):
        values = values.astype(BF16)
        for cc in range(NC):
            for xx in range(NX):
                for j in range(4):
                    first = block_row(t, cc, xx, j)
                    piece[t, cc, h, xx, 16 * j:16 * (j + 1)] = values[first:first + 16]

    def after_core(t, h):
        for xx in range(NX):
            total = piece[t, c, h, xx].astype(F32) + core_in[t, h, xx].astype(F32)
            mid[t, xx, h] = total.astype(BF16)

    def to_z(t, h, total):
        total = total.astype(BF16)
        for j in range(4):
            low[h, spot_z(x, t, j)] = total[16 * j:16 * (j + 1)]
        for j in range(4):
            @pl.when(z != spot_z(x, t, j))
            def _():
                z_copy(h, spot_z(x, t, j)).start()

    def start_ring(t):
        core_copy(t).wait_recv()
        for h in range(2):
            after_core(t, h)
        for h in range(2):
            relay_copy(t, h).start()
        for h in range(2):
            x_copy(t, 1 - h, h).start()

    def step_ring(t):
        for h in range(2):
            relay_copy(t, h).wait_recv()
            there = prev_x if h else next_x
            total = mid[t, there, h].astype(F32) + relay_in[t - 1, h].astype(F32)
            mid[t, there, h] = total.astype(BF16)
            x_copy(t, h, h).start()

    def end_ring(t):
        for h in range(2):
            x_copy(t, 0, h).wait_recv()
            x_copy(t, 1, h).wait_recv()
            total = mid[t, x, h].astype(F32) + x_in[t - 1, 0, h].astype(F32)
            to_z(t, h, total + x_in[t - 1, 1, h].astype(F32))

    def start_grid(h):
        core_half(h).wait_recv()
        after_core(GRID_TYPE, h)
        for d in (2, 1, 3):
            grid_copy(h, d).start()

    def end_grid(h):
        for d in range(1, NX):
            grid_copy(h, d).wait_recv()
        total = mid[GRID_TYPE, x, h].astype(F32)
        for d in range(1, NX):
            total = total + grid_in[h, d - 1].astype(F32)
        to_z(GRID_TYPE, h, total)

    sums = dot(pickt[GRID_ROWS:, :], actgp[...])
    mine[...] = sums[:MESH_ROWS, D:]
    terms = sums[:, D:].astype(BF16)
    tosend[...] = terms[MESH_ROWS:]
    west_copy().start()
    acts = sums[:, :D].T.astype(BF16)
    for h in range(2):
        put(OUT_TYPE, h, dot(acts, ct[:, h * HALF:(h + 1) * HALF]))
    core_copy(OUT_TYPE).start()
    for h in range(2):
        put(MESH_TYPE, h, dot(mlt[...], terms[:, h * HALF:(h + 1) * HALF]))
    core_copy(MESH_TYPE).start()

    def grid_side(first):
        def step(i, carry):
            rows = pl.ds(pl.multiple_of(i * 512, 512), 512)
            gpg[rows, :] = dot(pickt[rows, :], actgp[:, D:]).astype(BF16)
            return carry

        lax.fori_loop(first, first + 1, step, 0)

    grid_side(0)
    start_ring(OUT_TYPE)
    start_ring(MESH_TYPE)
    grid_side(1)
    for h in range(2):
        put(GRID_TYPE, h, dot(glt[...], gpg[:, h * HALF:(h + 1) * HALF]))
        core_half(h).start()

    def grid_grads(first):
        def step(i, carry):
            rows = pl.ds(pl.multiple_of(i * 512, 512), 512)
            gg[rows, :] = dot_bt(gpg[rows, :], wg[...]).astype(BF16)
            return carry

        lax.fori_loop(first, first + 1, step, 0)

    def store(i, source, goal):
        return pltpu.make_async_copy(source, goal, store_sem.at[i])

    step_ring(OUT_TYPE)
    step_ring(MESH_TYPE)
    start_grid(0)
    start_grid(1)
    grid_grads(0)
    hear(4)
    end_ring(OUT_TYPE)
    end_ring(MESH_TYPE)
    grid_grads(1)
    store(0, gg, gg_hbm).start()
    west_copy().wait_recv()
    mg[...] = dot_bt((mine[...] + west[...].astype(F32)).astype(BF16), wm[...]).astype(BF16)
    store(1, mg, mg_hbm).start()
    end_grid(0)
    end_grid(1)

    for h in range(2):
        whole(z_in.at[h], z_send.at[h], z_recv.at[h]).wait_recv()
        total = low[h, z].astype(F32)
        for s in range(NZ - 1):
            total = total + z_in[h, s].astype(F32)
        last[h] = total.astype(BF16)
        for d in (4, 3, 5, 2, 6, 1, 7):
            y_copy(h, (band + d) % NY, 0).start()

        @pl.when(moved)
        def _():
            y_copy(h, band, 1).start()

        @pl.when(jnp.logical_not(moved))
        def _():
            y_in[h, band] = last[h]

    for h in range(2):
        rest = y_in.at[h, pl.ds(1, NY - 1)]
        whole(rest, y_send.at[h, 0], y_recv.at[h, 0]).wait_recv()

        @pl.when(moved)
        def _():
            y_copy(h, band, 1).wait_recv()

        total = y_in[h, 0].astype(F32)
        for s in range(1, NY):
            total = total + y_in[h, s].astype(F32)
        wout[:, h * HALF:(h + 1) * HALF] = total
    store(2, wout, wgrad_hbm).start()

    east_copy(0, ml).wait_send()
    east_copy(1, ct).wait_send()
    west_copy().wait_send()
    for t in (MESH_TYPE, OUT_TYPE):
        core_copy(t).wait_send()
        for h in range(2):
            relay_copy(t, h).wait_send()
            x_copy(t, 0, h).wait_send()
            x_copy(t, 1, h).wait_send()
    for h in range(2):
        core_half(h).wait_send()
        for d in range(1, NX):
            grid_copy(h, d).wait_send()
        whole(z_in.at[h], z_send.at[h], z_recv.at[h]).wait_send()
        whole(y_in.at[h, pl.ds(1, NY - 1)], y_send.at[h, 0], y_recv.at[h, 0]).wait_send()

        @pl.when(moved)
        def _():
            y_copy(h, band, 1).wait_send()

    store(0, gg, gg_hbm).wait()
    store(1, mg, mg_hbm).wait()
    store(2, wout, wgrad_hbm).wait()


def hand_over(a, b, c, a_out, b_out, c_out, a_held, b_held, c_held, in_sem, out_sem):
    quarter = GRID_ROWS // 4
    parts = [(a.at[pl.ds(i * quarter, quarter)], a_held.at[pl.ds(i * quarter, quarter)],
              a_out.at[pl.ds(i * quarter, quarter)]) for i in range(4)]
    parts += [(b, b_held, b_out), (c, c_held, c_out)]
    reads = [pltpu.make_async_copy(source, held, in_sem.at[i]) for i, (source, held, _) in enumerate(parts)]
    writes = [pltpu.make_async_copy(held, goal, out_sem.at[i]) for i, (_, held, goal) in enumerate(parts)]
    for copy in reads:
        copy.start()
    for read, write in zip(reads, writes):
        read.wait()
        write.start()
    for copy in writes:
        copy.wait()


def on_device(
    grid_latent, mesh_latent, mesh_cotangent, w_grid, w_mesh, w_out, edge_source, edge_target, edge_count
):
    edges = (SLOTS // LANES, LANES)
    dma = pltpu.SemaphoreType.DMA
    vmem = pltpu.VMEM
    anywhere = pl.BlockSpec(memory_space=pl.ANY)
    results = (
        jax.ShapeDtypeStruct((GRID_ROWS, D), BF16),
        jax.ShapeDtypeStruct((MESH_ROWS, D), BF16),
        jax.ShapeDtypeStruct((16, D), F32),
    )
    made = pl.pallas_call(
        kernel,
        out_shape=results,
        in_specs=[anywhere] * 8 + [pl.BlockSpec(memory_space=pltpu.SMEM)],
        out_specs=[anywhere] * 3,
        scratch_shapes=[
            vmem((GRID_ROWS, D), BF16),
            vmem((D, GRID_ROWS), BF16),
            vmem((D, D), BF16),
            vmem((D, D), BF16),
            vmem((D, D), BF16),
            vmem((TABLE, D), BF16),
            vmem((D, TABLE), BF16),
            vmem((TABLE, D), BF16),
            vmem(edges, jnp.int32),
            vmem(edges, jnp.int32),
            vmem((SLOTS, GRID_ROWS + TABLE), BF16),
            vmem((GRID_ROWS + TABLE, SLOTS), BF16),
            vmem((GRID_ROWS, D), BF16),
            vmem((TABLE, 2 * D), BF16),
            vmem((SLOTS, D), F32),
            vmem((SLOTS, 2 * D), BF16),
            vmem((GRID_ROWS, D), BF16),
            vmem((GRID_ROWS, D), BF16),
            vmem((MESH_ROWS, D), BF16),
            vmem((MESH_ROWS, D), F32),
            vmem((MESH_ROWS, D), BF16),
            vmem((MESH_ROWS, D), BF16),
            vmem((3, NC, 2, NX, 64, HALF), BF16),
            vmem((3, 2, NX, 64, HALF), BF16),
            vmem((3, NX, 2, 64, HALF), BF16),
            vmem((2, 2, 64, HALF), BF16),
            vmem((2, 2, 2, 64, HALF), BF16),
            vmem((2, NX - 1, 64, HALF), BF16),
            vmem((2, NZ, 16, HALF), BF16),
            vmem((2, NZ - 1, 16, HALF), BF16),
            vmem((2, 16, HALF), BF16),
            vmem((2, NY, 16, HALF), BF16),
            vmem((16, D), F32),
            dma((8,)),
            dma((3,)),
            pltpu.SemaphoreType.REGULAR((ROUNDS,)),
            dma((2,)),
            dma((2,)),
            dma,
            dma,
            dma((3, 2)),
            dma((3, 2)),
            dma((2, 2)),
            dma((2, 2)),
            dma((2, 2, 2)),
            dma((2, 2, 2)),
            dma((2, NX - 1)),
            dma((2, NX - 1)),
            dma((2,)),
            dma((2,)),
            dma((2, 2)),
            dma((2, 2)),
        ],
        compiler_params=pltpu.CompilerParams(
            collective_id=0, has_side_effects=True, vmem_limit_bytes=56 * 1024 * 1024
        ),
        cost_estimate=pl.CostEstimate(flops=17_000_000_000, bytes_accessed=5_000_000, transcendentals=1_000_000),
    )(
        grid_latent, mesh_latent, mesh_cotangent, w_grid, w_mesh, w_out,
        edge_source.reshape(edges), edge_target.reshape(edges), edge_count,
    )
    return pl.pallas_call(
        hand_over,
        out_shape=results,
        in_specs=[anywhere] * 3,
        out_specs=[anywhere] * 3,
        scratch_shapes=[
            vmem((GRID_ROWS, D), BF16), vmem((MESH_ROWS, D), BF16), vmem((16, D), F32), dma((6,)), dma((6,)),
        ],
        cost_estimate=pl.CostEstimate(flops=0, bytes_accessed=2_400_000, transcendentals=0),
    )(*made)


def solution(mesh):
    in_specs = (
        P(("band", "lon"), None),
        P(("band", "lon"), None),
        P(("band", "lon"), None),
        P(),
        P(),
        P(),
        P(("band", "lon")),
        P(("band", "lon")),
        P(("band", "lon")),
    )
    out_specs = (P(("band", "lon"), None), P(("band", "lon"), None), P("lon", None))
    return jax.shard_map(
        on_device, mesh=mesh, in_specs=in_specs, out_specs=out_specs, check_vma=False
    )
```

```python
import jax
import jax.numpy as jnp
from jax import lax
from jax.experimental import pallas as pl
from jax.experimental.pallas import tpu as pltpu
from jax.sharding import PartitionSpec as P

MESH = pl.DeviceIdType.MESH
BF16 = jnp.bfloat16
F32 = jnp.float32

D = 512
HALF = 256
GRID_ROWS = 1024
MESH_ROWS = 128
TABLE = 2 * MESH_ROWS
SLOTS = 2048
LANES = 128
CHUNK = 512
NX, NY, NZ, NC = 4, 8, 12, 2
N_LON = NX * NZ * NC
ROUNDS = NZ // 2 - 1
GRID_TYPE, MESH_TYPE, OUT_TYPE = 0, 1, 2
SPOTS = (
    ((0, 0), (0, 1), (0, 2), (1, 0)),
    ((1, 1), (1, 2), (2, 0), (2, 1)),
    ((2, 2), (3, 0), (3, 1), (3, 2)),
)


def dot(a, b):
    return lax.dot_general(a, b, (((1,), (0,)), ((), ())), preferred_element_type=F32)


def dot_bt(a, b):
    return lax.dot_general(a, b, (((1,), (1,)), ((), ())), preferred_element_type=F32)


def lon_of(x, z, c):
    return (x * NZ + z) * NC + c


def spot_z(x, t, j):
    owner_x, group = SPOTS[t][j]
    return 4 * group + (x + NX - owner_x) % NX


def block_row(t, c, x, j):
    return 16 * (lon_of(SPOTS[t][j][0], spot_z(x, t, j), c) - 32 * t)


def kernel(
    gl_hbm, ml_hbm, ct_hbm, wg_hbm, wm_hbm, wo_hbm, src_hbm, tgt_hbm, cnt,
    gg_hbm, mg_hbm, wgrad_hbm,
    gl, glt, wg, wm, wo, ml, mlt, ct, src, tgt,
    pick, pickt, table, mtable, pre, actgp, gpg, gg, mg,
    mine, tosend, west,
    piece, core_in, mid, relay_in, x_in, grid_in, low, z_in, last, y_in, wout,
    load_sem, store_sem, token,
    east_send, east_recv, west_send, west_recv,
    core_send, core_recv, relay_send, relay_recv, x_send, x_recv, grid_send, grid_recv,
    z_send, z_recv, y_send, y_recv,
):
    band = lax.axis_index("band")
    lon = lax.axis_index("lon")
    x = lon // (NZ * NC)
    z = (lon // NC) % NZ
    c = lon % NC
    moved = z % NX != 0
    owner = lon_of((x + NZ - z) % NX, z, c)
    to_west = (band, (lon + N_LON - 1) % N_LON)
    to_east = (band, (lon + 1) % N_LON)
    mate = (band, lon_of(x, z, 1 - c))

    def load(i, source, target):
        return pltpu.make_async_copy(source, target, load_sem.at[i])

    loads = [
        load(0, ml_hbm, ml.at[pl.ds(0, MESH_ROWS)]),
        load(1, ct_hbm, ct.at[pl.ds(0, MESH_ROWS)]),
        load(2, src_hbm, src),
        load(3, tgt_hbm, tgt),
        load(4, gl_hbm, gl),
        load(5, wg_hbm, wg),
        load(6, wm_hbm, wm),
        load(7, wo_hbm, wo),
    ]
    for copy in loads:
        copy.start()

    barrier = pltpu.get_barrier_semaphore()

    def greet(device):
        pl.semaphore_signal(barrier, inc=1, device_id=device, device_id_type=MESH)

    greet(to_west)
    greet(to_east)
    greet(mate)
    for d in range(1, NX):
        greet((band, lon_of((x + d) % NX, z, c)))

    beside = [
        (band, lon_of(x, (z + 1) % NZ, c)),
        (band, lon_of(x, (z + NZ - 1) % NZ, c)),
        ((band + 1) % NY, lon),
        ((band + NY - 1) % NY, lon),
    ]
    for device in beside:
        greet(device)

    def tell(i):
        for device in beside:
            pl.semaphore_signal(token.at[i], inc=1, device_id=device, device_id_type=MESH)

    def hear(i):
        pl.semaphore_wait(token.at[i], len(beside))

    def east_copy(i, ref):
        return pltpu.make_async_remote_copy(
            src_ref=ref.at[pl.ds(0, MESH_ROWS)],
            dst_ref=ref.at[pl.ds(MESH_ROWS, MESH_ROWS)],
            send_sem=east_send.at[i],
            recv_sem=east_recv.at[i],
            device_id=to_west,
            device_id_type=MESH,
        )

    def west_copy():
        return pltpu.make_async_remote_copy(
            src_ref=tosend,
            dst_ref=west,
            send_sem=west_send,
            recv_sem=west_recv,
            device_id=to_east,
            device_id_type=MESH,
        )

    def core_copy(t):
        return pltpu.make_async_remote_copy(
            src_ref=piece.at[t, 1 - c],
            dst_ref=core_in.at[t],
            send_sem=core_send.at[t, 0],
            recv_sem=core_recv.at[t, 0],
            device_id=mate,
            device_id_type=MESH,
        )

    def core_half(h):
        return pltpu.make_async_remote_copy(
            src_ref=piece.at[GRID_TYPE, 1 - c, h],
            dst_ref=core_in.at[GRID_TYPE, h],
            send_sem=core_send.at[GRID_TYPE, h],
            recv_sem=core_recv.at[GRID_TYPE, h],
            device_id=mate,
            device_id_type=MESH,
        )

    next_x = (x + 1) % NX
    far_x = (x + 2) % NX
    prev_x = (x + 3) % NX

    def relay_copy(t, h):
        return pltpu.make_async_remote_copy(
            src_ref=mid.at[t, far_x, h],
            dst_ref=relay_in.at[t - 1, h],
            send_sem=relay_send.at[t - 1, h],
            recv_sem=relay_recv.at[t - 1, h],
            device_id=(band, lon_of(prev_x if h else next_x, z, c)),
            device_id_type=MESH,
        )

    def x_copy(t, way, h):
        there = prev_x if way else next_x
        return pltpu.make_async_remote_copy(
            src_ref=mid.at[t, there, h],
            dst_ref=x_in.at[t - 1, way, h],
            send_sem=x_send.at[t - 1, way, h],
            recv_sem=x_recv.at[t - 1, way, h],
            device_id=(band, lon_of(there, z, c)),
            device_id_type=MESH,
        )

    def grid_copy(h, d):
        there = (x + d) % NX
        return pltpu.make_async_remote_copy(
            src_ref=mid.at[GRID_TYPE, there, h],
            dst_ref=grid_in.at[h, d - 1],
            send_sem=grid_send.at[h, d - 1],
            recv_sem=grid_recv.at[h, d - 1],
            device_id=(band, lon_of(there, z, c)),
            device_id_type=MESH,
        )

    def z_copy(h, there):
        slot = (there + NZ - z + NZ - 1) % NZ
        return pltpu.make_async_remote_copy(
            src_ref=low.at[h, there],
            dst_ref=z_in.at[h, slot],
            send_sem=z_send.at[h],
            recv_sem=z_recv.at[h],
            device_id=(band, lon_of(x, there, c)),
            device_id_type=MESH,
        )

    def y_copy(h, y, i):
        return pltpu.make_async_remote_copy(
            src_ref=last.at[h],
            dst_ref=y_in.at[h, band],
            send_sem=y_send.at[h, i],
            recv_sem=y_recv.at[h, i],
            device_id=(y, owner),
            device_id_type=MESH,
        )

    def whole(ref, send, recv):
        return pltpu.make_async_remote_copy(
            src_ref=ref, dst_ref=ref, send_sem=send, recv_sem=recv,
            device_id=mate, device_id_type=MESH,
        )

    loads[0].wait()
    loads[1].wait()
    pl.semaphore_wait(barrier, 3 + (NX - 1) + len(beside))
    east_copy(0, ml).start()
    east_copy(1, ct).start()
    tell(0)

    loads[2].wait()
    loads[3].wait()
    slot = lax.broadcasted_iota(jnp.int32, (SLOTS // LANES, LANES), 0) * LANES
    slot = slot + lax.broadcasted_iota(jnp.int32, (SLOTS // LANES, LANES), 1)
    target = tgt[...]
    start = (band * N_LON + lon) * MESH_ROWS
    here = (target >= start) & (target < start + MESH_ROWS)
    row = jnp.where(here, target - start, MESH_ROWS + (target & (MESH_ROWS - 1)))
    tgt[...] = jnp.where(slot < cnt[0], row + GRID_ROWS, -1)

    across = lax.broadcasted_iota(jnp.int32, (LANES, LANES), 1).astype(jnp.int16)
    down = lax.broadcasted_iota(jnp.int32, (LANES, LANES), 0).astype(jnp.int16)

    def build(r):
        columns = slice(r * LANES, (r + 1) * LANES)
        sb = jnp.broadcast_to(src[r:r + 1, :], (LANES, LANES)).astype(jnp.int16)
        tb = jnp.broadcast_to(tgt[r:r + 1, :], (LANES, LANES)).astype(jnp.int16)
        st = sb.T
        tt = tb.T
        for k in range((GRID_ROWS + TABLE) // LANES):
            one = (sb if k < GRID_ROWS // LANES else tb) == down + jnp.int16(k * LANES)
            pickt[k * LANES:(k + 1) * LANES, columns] = jnp.where(one, jnp.ones((), BF16), jnp.zeros((), BF16))
            one = (st if k < GRID_ROWS // LANES else tt) == across + jnp.int16(k * LANES)
            pick[columns, k * LANES:(k + 1) * LANES] = jnp.where(one, jnp.ones((), BF16), jnp.zeros((), BF16))

    def build_chunk(i):
        for r in range(CHUNK // LANES):
            build(i * (CHUNK // LANES) + r)

    build_chunk(0)

    hear(0)
    tell(1)

    loads[4].wait()
    loads[5].wait()
    table[...] = dot(gl[...], wg[...]).astype(BF16)
    build_chunk(1)
    hear(1)
    tell(2)

    for first in range(0, SLOTS, CHUNK):
        pre[first:first + CHUNK, :] = dot(pick[first:first + CHUNK, :GRID_ROWS], table[...])
        if first + 2 * CHUNK < SLOTS:
            build_chunk(first // CHUNK + 2)
        else:
            turned = slice(GRID_ROWS * (first - SLOTS + 2 * CHUNK) // (2 * CHUNK), GRID_ROWS * (first - SLOTS + 3 * CHUNK) // (2 * CHUNK))
            glt[:, turned] = gl[turned, :].T
    hear(2)
    tell(3)


    loads[6].wait()
    loads[7].wait()
    east_copy(0, ml).wait_recv()
    east_copy(1, ct).wait_recv()
    mlt[...] = ml[...].T
    mtable[:, :D] = dot(ml[...], wm[...]).astype(BF16)
    mtable[:, D:] = dot_bt(ct[...], wo[...]).astype(BF16)

    for first in range(0, SLOTS, 512):
        rows = slice(first, first + 512)
        both = dot(pick[rows, GRID_ROWS:], mtable[...])
        value = pre[rows, :] + both[:, :D]
        sig = 0.5 * jnp.tanh(0.5 * value) + 0.5
        act = value * sig
        actgp[rows, :D] = act.astype(BF16)
        actgp[rows, D:] = (both[:, D:] * (sig + act * (1.0 - sig))).astype(BF16)

    hear(3)
    tell(4)

    def put(t, h, values):
        values = values.astype(BF16)
        for cc in range(NC):
            for xx in range(NX):
                for j in range(4):
                    first = block_row(t, cc, xx, j)
                    piece[t, cc, h, xx, 16 * j:16 * (j + 1)] = values[first:first + 16]

    def after_core(t, h):
        for xx in range(NX):
            total = piece[t, c, h, xx].astype(F32) + core_in[t, h, xx].astype(F32)
            mid[t, xx, h] = total.astype(BF16)

    def to_z(t, h, total):
        total = total.astype(BF16)
        for j in range(4):
            low[h, spot_z(x, t, j)] = total[16 * j:16 * (j + 1)]
        for j in range(4):
            @pl.when(z != spot_z(x, t, j))
            def _():
                z_copy(h, spot_z(x, t, j)).start()

    def start_ring(t):
        core_copy(t).wait_recv()
        for h in range(2):
            after_core(t, h)
        for h in range(2):
            relay_copy(t, h).start()
        for h in range(2):
            x_copy(t, 1 - h, h).start()

    def step_ring(t):
        for h in range(2):
            relay_copy(t, h).wait_recv()
            there = prev_x if h else next_x
            total = mid[t, there, h].astype(F32) + relay_in[t - 1, h].astype(F32)
            mid[t, there, h] = total.astype(BF16)
            x_copy(t, h, h).start()

    def end_ring(t):
        for h in range(2):
            x_copy(t, 0, h).wait_recv()
            x_copy(t, 1, h).wait_recv()
            total = mid[t, x, h].astype(F32) + x_in[t - 1, 0, h].astype(F32)
            to_z(t, h, total + x_in[t - 1, 1, h].astype(F32))

    def start_grid(h):
        core_half(h).wait_recv()
        after_core(GRID_TYPE, h)
        for d in (2, 1, 3):
            grid_copy(h, d).start()

    def end_grid(h):
        for d in range(1, NX):
            grid_copy(h, d).wait_recv()
        total = mid[GRID_TYPE, x, h].astype(F32)
        for d in range(1, NX):
            total = total + grid_in[h, d - 1].astype(F32)
        to_z(GRID_TYPE, h, total)

    sums = dot(pickt[GRID_ROWS:, :], actgp[...])
    mine[...] = sums[:MESH_ROWS, D:]
    terms = sums[:, D:].astype(BF16)
    tosend[...] = terms[MESH_ROWS:]
    west_copy().start()
    acts = sums[:, :D].T.astype(BF16)
    for h in range(2):
        put(OUT_TYPE, h, dot(acts, ct[:, h * HALF:(h + 1) * HALF]))
    core_copy(OUT_TYPE).start()
    for h in range(2):
        put(MESH_TYPE, h, dot(mlt[...], terms[:, h * HALF:(h + 1) * HALF]))
    core_copy(MESH_TYPE).start()

    def grid_side(i):
        rows = slice(i * CHUNK, (i + 1) * CHUNK)
        gpg[rows, :] = dot(pickt[rows, :], actgp[:, D:]).astype(BF16)

    grid_side(0)
    start_ring(OUT_TYPE)
    start_ring(MESH_TYPE)
    grid_side(1)
    for h in range(2):
        put(GRID_TYPE, h, dot(glt[...], gpg[:, h * HALF:(h + 1) * HALF]))
        core_half(h).start()

    def grid_grads(first):
        def step(i, carry):
            rows = pl.ds(pl.multiple_of(i * 512, 512), 512)
            gg[rows, :] = dot_bt(gpg[rows, :], wg[...]).astype(BF16)
            return carry

        lax.fori_loop(first, first + 1, step, 0)

    def store(i, source, goal):
        return pltpu.make_async_copy(source, goal, store_sem.at[i])

    step_ring(OUT_TYPE)
    step_ring(MESH_TYPE)
    start_grid(0)
    start_grid(1)
    grid_grads(0)
    hear(4)
    end_ring(OUT_TYPE)
    end_ring(MESH_TYPE)
    end_grid(0)
    end_grid(1)
    grid_grads(1)
    store(0, gg, gg_hbm).start()
    west_copy().wait_recv()
    mg[...] = dot_bt((mine[...] + west[...].astype(F32)).astype(BF16), wm[...]).astype(BF16)
    store(1, mg, mg_hbm).start()

    for h in range(2):
        whole(z_in.at[h], z_send.at[h], z_recv.at[h]).wait_recv()
        total = low[h, z].astype(F32)
        for s in range(NZ - 1):
            total = total + z_in[h, s].astype(F32)
        last[h] = total.astype(BF16)
        for d in (4, 3, 5, 2, 6, 1, 7):
            y_copy(h, (band + d) % NY, 0).start()

        @pl.when(moved)
        def _():
            y_copy(h, band, 1).start()

        @pl.when(jnp.logical_not(moved))
        def _():
            y_in[h, band] = last[h]

    for h in range(2):
        rest = y_in.at[h, pl.ds(1, NY - 1)]
        whole(rest, y_send.at[h, 0], y_recv.at[h, 0]).wait_recv()

        @pl.when(moved)
        def _():
            y_copy(h, band, 1).wait_recv()

        total = y_in[h, 0].astype(F32)
        for s in range(1, NY):
            total = total + y_in[h, s].astype(F32)
        wout[:, h * HALF:(h + 1) * HALF] = total
    store(2, wout, wgrad_hbm).start()

    east_copy(0, ml).wait_send()
    east_copy(1, ct).wait_send()
    west_copy().wait_send()
    for t in (MESH_TYPE, OUT_TYPE):
        core_copy(t).wait_send()
        for h in range(2):
            relay_copy(t, h).wait_send()
            x_copy(t, 0, h).wait_send()
            x_copy(t, 1, h).wait_send()
    for h in range(2):
        core_half(h).wait_send()
        for d in range(1, NX):
            grid_copy(h, d).wait_send()
        whole(z_in.at[h], z_send.at[h], z_recv.at[h]).wait_send()
        whole(y_in.at[h, pl.ds(1, NY - 1)], y_send.at[h, 0], y_recv.at[h, 0]).wait_send()

        @pl.when(moved)
        def _():
            y_copy(h, band, 1).wait_send()

    store(0, gg, gg_hbm).wait()
    store(1, mg, mg_hbm).wait()
    store(2, wout, wgrad_hbm).wait()


def hand_over(a, b, c, a_out, b_out, c_out, a_held, b_held, c_held, in_sem, out_sem):
    quarter = GRID_ROWS // 4
    parts = [(a.at[pl.ds(i * quarter, quarter)], a_held.at[pl.ds(i * quarter, quarter)],
              a_out.at[pl.ds(i * quarter, quarter)]) for i in range(4)]
    parts += [(b, b_held, b_out), (c, c_held, c_out)]
    reads = [pltpu.make_async_copy(source, held, in_sem.at[i]) for i, (source, held, _) in enumerate(parts)]
    writes = [pltpu.make_async_copy(held, goal, out_sem.at[i]) for i, (_, held, goal) in enumerate(parts)]
    for copy in reads:
        copy.start()
    for read, write in zip(reads, writes):
        read.wait()
        write.start()
    for copy in writes:
        copy.wait()


def on_device(
    grid_latent, mesh_latent, mesh_cotangent, w_grid, w_mesh, w_out, edge_source, edge_target, edge_count
):
    edges = (SLOTS // LANES, LANES)
    dma = pltpu.SemaphoreType.DMA
    vmem = pltpu.VMEM
    anywhere = pl.BlockSpec(memory_space=pl.ANY)
    results = (
        jax.ShapeDtypeStruct((GRID_ROWS, D), BF16),
        jax.ShapeDtypeStruct((MESH_ROWS, D), BF16),
        jax.ShapeDtypeStruct((16, D), F32),
    )
    made = pl.pallas_call(
        kernel,
        out_shape=results,
        in_specs=[anywhere] * 8 + [pl.BlockSpec(memory_space=pltpu.SMEM)],
        out_specs=[anywhere] * 3,
        scratch_shapes=[
            vmem((GRID_ROWS, D), BF16),
            vmem((D, GRID_ROWS), BF16),
            vmem((D, D), BF16),
            vmem((D, D), BF16),
            vmem((D, D), BF16),
            vmem((TABLE, D), BF16),
            vmem((D, TABLE), BF16),
            vmem((TABLE, D), BF16),
            vmem(edges, jnp.int32),
            vmem(edges, jnp.int32),
            vmem((SLOTS, GRID_ROWS + TABLE), BF16),
            vmem((GRID_ROWS + TABLE, SLOTS), BF16),
            vmem((GRID_ROWS, D), BF16),
            vmem((TABLE, 2 * D), BF16),
            vmem((SLOTS, D), F32),
            vmem((SLOTS, 2 * D), BF16),
            vmem((GRID_ROWS, D), BF16),
            vmem((GRID_ROWS, D), BF16),
            vmem((MESH_ROWS, D), BF16),
            vmem((MESH_ROWS, D), F32),
            vmem((MESH_ROWS, D), BF16),
            vmem((MESH_ROWS, D), BF16),
            vmem((3, NC, 2, NX, 64, HALF), BF16),
            vmem((3, 2, NX, 64, HALF), BF16),
            vmem((3, NX, 2, 64, HALF), BF16),
            vmem((2, 2, 64, HALF), BF16),
            vmem((2, 2, 2, 64, HALF), BF16),
            vmem((2, NX - 1, 64, HALF), BF16),
            vmem((2, NZ, 16, HALF), BF16),
            vmem((2, NZ - 1, 16, HALF), BF16),
            vmem((2, 16, HALF), BF16),
            vmem((2, NY, 16, HALF), BF16),
            vmem((16, D), F32),
            dma((8,)),
            dma((3,)),
            pltpu.SemaphoreType.REGULAR((ROUNDS,)),
            dma((2,)),
            dma((2,)),
            dma,
            dma,
            dma((3, 2)),
            dma((3, 2)),
            dma((2, 2)),
            dma((2, 2)),
            dma((2, 2, 2)),
            dma((2, 2, 2)),
            dma((2, NX - 1)),
            dma((2, NX - 1)),
            dma((2,)),
            dma((2,)),
            dma((2, 2)),
            dma((2, 2)),
        ],
        compiler_params=pltpu.CompilerParams(
            collective_id=0, has_side_effects=True, vmem_limit_bytes=56 * 1024 * 1024
        ),
        cost_estimate=pl.CostEstimate(flops=17_000_000_000, bytes_accessed=5_000_000, transcendentals=1_000_000),
    )(
        grid_latent, mesh_latent, mesh_cotangent, w_grid, w_mesh, w_out,
        edge_source.reshape(edges), edge_target.reshape(edges), edge_count,
    )
    return pl.pallas_call(
        hand_over,
        out_shape=results,
        in_specs=[anywhere] * 3,
        out_specs=[anywhere] * 3,
        scratch_shapes=[
            vmem((GRID_ROWS, D), BF16), vmem((MESH_ROWS, D), BF16), vmem((16, D), F32), dma((6,)), dma((6,)),
        ],
        cost_estimate=pl.CostEstimate(flops=0, bytes_accessed=2_400_000, transcendentals=0),
    )(*made)


def solution(mesh):
    in_specs = (
        P(("band", "lon"), None),
        P(("band", "lon"), None),
        P(("band", "lon"), None),
        P(),
        P(),
        P(),
        P(("band", "lon")),
        P(("band", "lon")),
        P(("band", "lon")),
    )
    out_specs = (P(("band", "lon"), None), P(("band", "lon"), None), P("lon", None))
    return jax.shard_map(
        on_device, mesh=mesh, in_specs=in_specs, out_specs=out_specs, check_vma=False
    )
```
